768 devices in a mesh: wide: 32 (over z_lo, y), rep: 24 (over z_hi, x, core).
Axes of the slice: x: 4, y: 8, z: 12 (z_hi: 3, z_lo: 4; z = z_hi * 4 + z_lo), core: 2. Of those that a mesh axis runs over, the one named last changes fastest.
Arguments:
- features: bfloat16 [98304, 128], P(('wide', 'rep')), may hold values from -6 to 6
- weight: bfloat16 [128, 256], replicated, may hold values from -0.5 to 0.5
- cotangent: bfloat16 [98304, 256], P(('wide', 'rep')), may hold values from -6 to 6
- tile_values: bfloat16 [32, 24, 32, 4, 128, 128], P('wide', 'rep'), may hold values from -0.09375 to 0.09375
- tile_rows: int32 [32, 24, 32, 4], P('wide', 'rep'), may hold values from 0 to 23, as said below
- tile_counts: int32 [32, 24, 32], P('wide', 'rep'), may hold values from 0 to 4, as said below
Outputs:
- output: bfloat16 [98304, 256], P(('wide', 'rep'))
- weight_grad: float32 [128, 256], replicated
- feature_grad: bfloat16 [98304, 128], P(('wide', 'rep'))
The draws below stay inside these ranges and needn't reach their ends.
Inputs may be any that keep to these rules, and one draw needn't show every extreme that they name: `tile_rows`: the 4 row tiles of each list are distinct. `tile_counts`: in some row block every list is full.
All inputs are finite; a program needn't handle non-finite values.
Results may differ from the reference program's by a relative error of at most 0.0065.
Values may be sent and summed in bfloat16 or wider, within the bound.
A program may use at most 32 MiB of HBM per device.

```python
import jax
import jax.numpy as jnp
from jax import lax

F = 128
HID = 256
TILE = 128
KT = 4
NODES = 98304
N_WIDE = 32
N_REP = 24


def draw_tile_rows(key, part):
    key = jax.random.fold_in(key, 11)
    scores = jax.random.randint(key, (N_WIDE, N_REP, N_WIDE, N_REP), 0, 2 ** 20) * N_REP
    scores = scores + jnp.arange(N_REP, dtype=jnp.int32)
    return jnp.argsort(scores, axis=-1)[..., :KT].astype(jnp.int32)


def draw_tile_counts(key, part):
    key = jax.random.fold_in(key, 23)
    base_key, dense_key, forced_key = jax.random.split(key, 3)
    base_counts = jax.random.randint(base_key, (N_WIDE, N_REP, N_WIDE), 0, KT // 2 + 1)
    heavy_rows = jax.random.randint(dense_key, (N_WIDE,), 0, 4) == 0
    pinned_row = jnp.arange(N_WIDE, dtype=jnp.int32) == jax.random.randint(forced_key, (), 0, N_WIDE)
    full_rows = (heavy_rows | pinned_row)[:, None, None]
    return jnp.where(full_rows, KT, base_counts).astype(jnp.int32)


def levels(rng, shape, cuts, low, largest):
    def one(dim, shards_of):
        steps = jax.random.uniform(jax.random.fold_in(jax.random.fold_in(rng, 6), dim), (shards_of,), jnp.float32, low / len(cuts), largest / len(cuts))
        return jnp.repeat(jnp.exp(steps), shape[dim] // shards_of).reshape((-1,) + (1,) * (len(shape) - dim - 1))

    loudness = one(*cuts[0])
    for cut in cuts[1:]:
        loudness = loudness * one(*cut)
    return loudness


def centred(own_key, dims, spread, bound, shards=(), kind=jnp.bfloat16):
    entries = spread * jax.random.normal(own_key, dims, jnp.float32)
    if shards:
        entries = entries * levels(own_key, dims, shards, -0.22, 0.18)
    return jnp.clip(entries, -bound, bound).astype(kind)


def setup_inputs(seed: int = 0) -> dict:
    streams_of = jax.random.split(jax.random.key(seed), 7)
    return {
        "features": centred(streams_of[0], (NODES, F), 1.0, 6.0, ((0, 768),)),
        "weight": centred(streams_of[1], (F, HID), F ** -0.5, 0.5),
        "cotangent": centred(streams_of[2], (NODES, HID), 1.0, 6.0, ((0, 768),)),
        "tile_values": centred(streams_of[3], (N_WIDE, N_REP, N_WIDE, KT, TILE, TILE), (TILE * N_WIDE) ** -0.5, 0.09375, ((0, 32), (1, 24))),
        "tile_rows": draw_tile_rows(jax.random.fold_in(streams_of[6], 71), 0),
        "tile_counts": draw_tile_counts(jax.random.fold_in(streams_of[6], 71), 0),
    }


def silu_slope(hidden):
    sig = jax.nn.sigmoid(hidden)
    return sig * (1.0 + hidden * (1.0 - sig))

def reference(features, weight, cotangent, tile_values, tile_rows, tile_counts):
    highest = lax.Precision.HIGHEST
    feature_tiles = features.reshape(N_WIDE, N_REP, TILE, F).astype(jnp.float32)
    slot_index = jnp.arange(KT, dtype=jnp.int32)
    live_mask = slot_index < tile_counts[..., None]
    row_index = jnp.arange(N_REP, dtype=jnp.int32)
    placement = ((tile_rows[..., None] == row_index) & live_mask[..., None]).astype(jnp.float32)

    def forward_block(inputs):
        block_values, block_map = inputs
        products = jnp.einsum('jckab,cjbf->jckaf', block_values.astype(jnp.float32), feature_tiles, precision=highest)
        return jnp.einsum('jckr,jckaf->raf', block_map, products, precision=highest)
    partial_value = lax.map(forward_block, (tile_values, placement))
    aggregated = partial_value.reshape(NODES, F).astype(jnp.bfloat16)
    hidden = jnp.dot(aggregated, weight, preferred_element_type=jnp.float32)
    output = jax.nn.silu(hidden).astype(jnp.bfloat16)
    grad_hidden = (cotangent.astype(jnp.float32) * silu_slope(hidden)).astype(jnp.bfloat16)
    weight_grad = jnp.dot(aggregated.T, grad_hidden, preferred_element_type=jnp.float32) / jnp.sqrt(jnp.float32(NODES))
    grad_aggregated = jnp.dot(grad_hidden, weight.T, preferred_element_type=jnp.float32).astype(jnp.bfloat16)
    grad_tiles = grad_aggregated.reshape(N_WIDE, N_REP, TILE, F).astype(jnp.float32)

    def backward_block(accumulated, inputs):
        block_values, block_map, block_grads = inputs
        chosen_entries = jnp.einsum('jckr,raf->jckaf', block_map, block_grads, precision=highest)
        contribution = jnp.einsum('jckab,jckaf->cjbf', block_values.astype(jnp.float32), chosen_entries, precision=highest)
        return (accumulated + contribution, None)
    start_value = jnp.zeros((N_WIDE, N_REP, TILE, F), jnp.float32)
    accumulated, _ = lax.scan(backward_block, start_value, (tile_values, placement, grad_tiles))
    feature_grad = accumulated.reshape(NODES, F).astype(jnp.bfloat16)
    return (output, weight_grad, feature_grad)
```

```python
import math

import jax
import jax.numpy as jnp
from jax import lax
from jax.experimental import pallas as pl
from jax.experimental.pallas import tpu as pltpu
from jax.sharding import PartitionSpec as P

MESH = pl.DeviceIdType.MESH
T = 128
NY, NZL, NZH, NX = 8, 4, 3, 4
N_WIDE, N_REP, KT = 32, 24, 4
BF = jnp.bfloat16
F32 = jnp.float32
X_ORDER = (2, 1, 3)


def place():
    wide = lax.axis_index("wide")
    rep = lax.axis_index("rep")
    y, zl = lax.rem(wide, NY), wide // NY
    core, x, zh = lax.rem(rep, 2), lax.rem(rep // 2, NX), rep // (2 * NX)
    return x, y, zl, zh, core


def kernel(
    feat, weight, cot, tiles_hbm, table,
    out_ref, wgrad_ref, fgrad_ref,
    tiles, xs, tot, sib_s, sib_r, x_s, x_r, z_s, z_r, g, y_s, y_r, f_s, f_r,
    w_t, w_r1, w_a, w_r2, w_c, w_d, w_e, w_o,
    tile_sem, ag_zs, ag_ys, ag_r, sib_ss, sib_rs, x_ss, x_rs, z_ss, z_rs,
    g_ss, g_rs, y_ss, y_rs, f_ss, f_rs, w_ss, w_rs,
):
    x, y, zl, zh, core = place()

    def dev(x=x, y=y, zl=zl, zh=zh, core=core):
        return (zl * NY + y, zh * (2 * NX) + x * 2 + core)

    def up(v, by, n):
        return lax.rem(v + by, n)

    sibling = dev(core=1 - core)

    def send(src, dst, ss, rs, to):
        pltpu.make_async_remote_copy(
            src_ref=src, dst_ref=dst, send_sem=ss, recv_sem=rs,
            device_id=to, device_id_type=MESH,
        ).start()

    def wait_recv(dst, rs):
        pltpu.make_async_remote_copy(
            src_ref=dst, dst_ref=dst, send_sem=rs, recv_sem=rs,
            device_id=sibling, device_id_type=MESH,
        ).wait_recv()

    def wait_send(src, ss):
        pltpu.make_async_remote_copy(
            src_ref=src, dst_ref=src, send_sem=ss, recv_sem=ss,
            device_id=sibling, device_id_type=MESH,
        ).wait_send()

    load = pltpu.make_async_copy(tiles_hbm, tiles, tile_sem)
    load.start()

    barrier = pltpu.get_barrier_semaphore()
    partners = [sibling]
    partners += [dev(x=up(x, d, NX)) for d in range(1, NX)]
    partners += [dev(y=up(y, d, NY)) for d in range(1, NY)]
    partners += [dev(zl=up(zl, d, NZL)) for d in range(1, NZL)]
    partners += [dev(zh=up(zh, d, NZH)) for d in range(1, NZH)]
    for partner in partners:
        pl.semaphore_signal(barrier, inc=1, device_id=partner, device_id_type=MESH)

    own = zl * NY + y
    xs[own] = feat[...]
    tot[N_WIDE * KT] = jnp.zeros((T, T), F32)
    g[N_REP] = jnp.zeros((T, T), BF)
    pl.semaphore_wait(barrier, len(partners))

    y_next, y_prev = dev(y=up(y, 1, NY)), dev(y=up(y, NY - 1, NY))

    def block(d, dy):
        return up(zl, d, NZL) * NY + up(y, dy, NY)

    def forward_up(h, d, c):
        send(xs.at[c], xs.at[c], ag_ys.at[0, h, d], ag_r.at[c], y_next)

    def forward_down(h, d, c):
        send(xs.at[c], xs.at[c], ag_ys.at[1, h, d], ag_r.at[c], y_prev)

    for d in range(1, NZL):
        send(xs.at[own], xs.at[own], ag_zs.at[d - 1], ag_r.at[own], dev(zl=up(zl, d, NZL)))
    forward_up(0, 0, own)
    forward_down(0, 0, own)
    load.wait()

    def process(rank, c):
        product = jnp.dot(
            tiles[c].reshape(KT * T, T), xs[c], preferred_element_type=F32
        )
        for k in range(KT):
            before = table[c * KT + k]
            tot[rank * KT + k] = product[k * T:(k + 1) * T] + tot[before]

    process(0, own)

    def z_step(d, carry):
        c = block(d, 0)
        wait_recv(xs.at[c], ag_r.at[c])
        forward_up(0, d, c)
        forward_down(0, d, c)
        process(d, c)
        return carry

    lax.fori_loop(1, NZL, z_step, 0)

    def y_step(step, carry):
        h, d = step // NZL + 1, lax.rem(step, NZL)
        c = block(d, NY - h)
        wait_recv(xs.at[c], ag_r.at[c])

        @pl.when((h < 3) | (d < 2))
        def _():
            forward_up(h, d, c)

        e = block(d, h)
        wait_recv(xs.at[e], ag_r.at[e])

        @pl.when((h < 3) | (d >= 2))
        def _():
            forward_down(h, d, e)

        process(NZL + 2 * step, c)
        process(NZL + 2 * step + 1, e)
        return carry

    lax.fori_loop(0, 3 * NZL, y_step, 0)

    def last_step(d, carry):
        c = block(d, 4)
        wait_recv(xs.at[c], ag_r.at[c])
        process(28 + d, c)
        return carry

    lax.fori_loop(0, NZL, last_step, 0)

    def part(zh_to, x_to, core_to):
        r = zh_to * (2 * NX) + x_to * 2 + core_to
        return tot[table[2 * N_WIDE * KT + r]]

    for n, dx in enumerate(X_ORDER + (0,)):
        for q in range(NZH):
            sib_s[n, q] = part(q, up(x, dx, NX), 1 - core)
        send(sib_s.at[n], sib_r.at[n], sib_ss.at[n], sib_rs.at[n], sibling)
    for n, dx in enumerate(X_ORDER):
        wait_recv(sib_r.at[n], sib_rs.at[n])
        for q in range(NZH):
            x_s[n, q] = (part(q, up(x, dx, NX), core) + sib_r[n, q]).astype(BF)
        send(x_s.at[n], x_r.at[n], x_ss.at[n], x_rs.at[n], dev(x=up(x, dx, NX)))
    wait_recv(sib_r.at[3], sib_rs.at[3])
    for n in range(3):
        wait_recv(x_r.at[n], x_rs.at[n])

    def column_sum(q):
        value = part(q, x, core) + sib_r[3, q]
        for n in range(3):
            value = value + x_r[n, q].astype(F32)
        return value

    for n in range(2):
        q = up(zh, n + 1, NZH)
        z_s[n] = column_sum(q).astype(BF)
        send(z_s.at[n], z_r.at[n], z_ss.at[n], z_rs.at[n], dev(zh=q))
    total = column_sum(zh)
    for n in range(2):
        wait_recv(z_r.at[n], z_rs.at[n])
        total = total + z_r[n].astype(F32)

    agg = total.astype(BF)
    hidden = jnp.dot(agg, weight[...], preferred_element_type=F32)
    sig = jax.nn.sigmoid(hidden)
    grad_hidden = (cot[...].astype(F32) * (sig * (1.0 + hidden * (1.0 - sig)))).astype(BF)
    grad_t = lax.dot_general(
        weight[...], grad_hidden, (((1,), (1,)), ((), ())), preferred_element_type=F32
    )
    mine = zh * (2 * NX) + x * 2 + core
    g[mine] = grad_t.astype(BF)

    def g_send(n, r, to):
        send(g.at[r], g.at[r], g_ss.at[n], g_rs.at[r], to)

    for n in range(2):
        g_send(n, mine, dev(zh=up(zh, n + 1, NZH)))
    for n, dx in enumerate(X_ORDER):
        g_send(2 + n, mine, dev(x=up(x, dx, NX)))
    g_send(5, mine, sibling)

    out_ref[...] = (hidden * sig).astype(BF)
    w_t[...] = lax.dot_general(
        agg, grad_hidden, (((0,), (0,)), ((), ())), preferred_element_type=F32
    )
    half = T // 2
    chunk = half // NX
    mine_half = pl.ds(pl.multiple_of(core * half, half), half)
    other_half = pl.ds(pl.multiple_of((1 - core) * half, half), half)
    send(w_t.at[other_half], w_r1, w_ss.at[0], w_rs.at[0], sibling)

    for n in range(2):
        r = up(zh, 2 - n, NZH) * (2 * NX) + x * 2 + core
        wait_recv(g.at[r], g_rs.at[r])
        for m, dx in enumerate(X_ORDER):
            g_send(6 + 4 * n + m, r, dev(x=up(x, dx, NX)))
        g_send(6 + 4 * n + 3, r, sibling)

    wait_recv(w_r1, w_rs.at[0])
    w_a[...] = w_t[mine_half] + w_r1[...]

    def chunk_of(v):
        return pl.ds(pl.multiple_of(v * chunk, chunk), chunk)

    for n, dx in enumerate(X_ORDER):
        to = up(x, dx, NX)
        send(w_a.at[chunk_of(to)], w_r2.at[n], w_ss.at[1 + n], w_rs.at[1 + n], dev(x=to))

    for q in range(NZH):
        for n, dx in enumerate(X_ORDER):
            r = up(zh, NZH - q, NZH) * (2 * NX) + up(x, NX - dx, NX) * 2 + core
            wait_recv(g.at[r], g_rs.at[r])
            g_send(14 + 3 * q + n, r, sibling)

    w_sum = w_a[chunk_of(x)]
    for n in range(3):
        wait_recv(w_r2.at[n], w_rs.at[1 + n])
        w_sum = w_sum + w_r2[n]
    w_c[y] = w_sum
    for n in range(1, NY):
        send(w_c.at[y], w_c.at[y], w_ss.at[3 + n], w_rs.at[4 + y], dev(y=up(y, n, NY)))

    def sib_wait(n, carry):
        r = n * 2 + 1 - core
        wait_recv(g.at[r], g_rs.at[r])
        return carry

    lax.fori_loop(0, N_REP // 2, sib_wait, 0)

    def term(c):
        left = jnp.concatenate(
            [g[table[N_WIDE * KT + c * KT + k]] for k in range(KT)], axis=1
        )
        return jnp.dot(left, tiles[c].reshape(KT * T, T), preferred_element_type=F32)

    def y_send(side, h, d, value):
        y_s[side, h - 1, d] = value.astype(BF)
        send(
            y_s.at[side, h - 1, d], y_r.at[side, h - 1, d],
            y_ss.at[side, h - 1, d], y_rs.at[side, h - 1, d],
            y_next if side == 0 else y_prev,
        )

    def arrived(side, h, d):
        wait_recv(y_r.at[side, h, d], y_rs.at[side, h, d])
        return y_r[side, h, d].astype(F32)

    def first(d, carry):
        y_send(0, 4, d, term(block(d, 4)))
        y_send(1, 4, d + 2, term(block(d + 2, 4)))
        return carry

    lax.fori_loop(0, 2, first, 0)

    def second(d, carry):
        y_send(0, 3, d + 2, term(block(d + 2, 3)))
        y_send(1, 3, d, term(block(d, NY - 3)))
        return carry

    lax.fori_loop(0, 2, second, 0)

    def third(d, carry):
        own_up = term(block(d, 3))
        own_down = term(block(d + 2, NY - 3))
        y_send(0, 3, d, own_up + arrived(0, 3, d))
        y_send(1, 3, d + 2, own_down + arrived(1, 3, d + 2))
        return carry

    lax.fori_loop(0, 2, third, 0)

    def ring(h):
        def body(d, carry):
            own_up = term(block(d, h))
            own_down = term(block(d, NY - h))
            y_send(0, h, d, own_up + arrived(0, h, d))
            y_send(1, h, d, own_down + arrived(1, h, d))
            return carry

        lax.fori_loop(0, NZL, body, 0)

    def spread_sum(buf, base, me, n):
        def wait_one(i, carry):
            @pl.when(i != me)
            def _():
                wait_recv(buf.at[i], w_rs.at[base + i])
            return carry

        lax.fori_loop(0, n, wait_one, 0)
        value = buf[0]
        for i in range(1, n):
            value = value + buf[i]
        return value

    w_d[zl] = spread_sum(w_c, 4, y, NY)
    for n in range(1, NZL):
        send(w_d.at[zl], w_d.at[zl], w_ss.at[10 + n], w_rs.at[12 + zl], dev(zl=up(zl, n, NZL)))

    ring(2)

    w_e[zh] = spread_sum(w_d, 12, zl, NZL)
    for n in range(1, NZH):
        send(w_e.at[zh], w_e.at[zh], w_ss.at[13 + n], w_rs.at[16 + zh], dev(zh=up(zh, n, NZH)))

    ring(1)

    w_own = spread_sum(w_e, 16, zh, NZH) * (1.0 / math.sqrt(N_WIDE * N_REP * T))
    w_o[core, x] = w_own
    for n in range(1, NX):
        send(w_o.at[core, x], w_o.at[core, x], w_ss.at[15 + n], w_rs.at[19 + x], dev(x=up(x, n, NX)))

    def last(d, carry):
        value = term(block(d, 0)) + arrived(0, 0, d)
        f_s[d - 1] = (value + arrived(1, 0, d)).astype(BF)
        send(f_s.at[d - 1], f_r.at[d - 1], f_ss.at[d - 1], f_rs.at[d - 1], dev(zl=up(zl, d, NZL)))
        return carry

    lax.fori_loop(1, NZL, last, 0)
    value = term(block(0, 0)) + arrived(0, 0, 0) + arrived(1, 0, 0)

    def gathered(i, carry):
        @pl.when(i != x)
        def _():
            wait_recv(w_o.at[core, i], w_rs.at[19 + i])
        return carry

    lax.fori_loop(0, NX, gathered, 0)
    send(w_o.at[core], w_o.at[core], w_ss.at[19], w_rs.at[23], sibling)

    for n in range(3):
        wait_recv(f_r.at[n], f_rs.at[n])
        value = value + f_r[n].astype(F32)
    fgrad_ref[...] = value.T.astype(BF)
    wait_recv(w_o.at[1 - core], w_rs.at[23])
    wgrad_ref[...] = w_o[...].reshape(T, 2 * T)

    for n in range(3):
        wait_send(xs.at[0], ag_zs.at[n])
    for n in range(3):
        wait_send(x_s.at[n], x_ss.at[n])
        wait_send(f_s.at[n], f_ss.at[n])
    for n in range(4):
        wait_send(sib_s.at[n], sib_ss.at[n])
    for n in range(2):
        wait_send(z_s.at[n], z_ss.at[n])

    def drain(step, carry):
        h, d = step // NZL, lax.rem(step, NZL)

        @pl.when((h < 3) | (d < 2))
        def _():
            wait_send(xs.at[0], ag_ys.at[0, h, d])
            wait_send(y_s.at[0, h, d], y_ss.at[0, h, d])

        @pl.when((h < 3) | (d >= 2))
        def _():
            wait_send(xs.at[0], ag_ys.at[1, h, d])
            wait_send(y_s.at[1, h, d], y_ss.at[1, h, d])

        return carry

    lax.fori_loop(0, 4 * NZL, drain, 0)

    def drain_g(n, carry):
        wait_send(g.at[0], g_ss.at[n])
        return carry

    lax.fori_loop(0, 23, drain_g, 0)
    wait_send(w_r1, w_ss.at[0])

    def drain_w(n, carry):
        wait_send(w_r2.at[0], w_ss.at[n])
        return carry

    lax.fori_loop(1, 19, drain_w, 0)
    wait_send(w_o.at[core], w_ss.at[19])


def make_table(rows, counts):
    x, y, zl, zh, core = place()
    c = jnp.arange(N_WIDE, dtype=jnp.int32)
    d = (c // NY - zl) % NZL
    dy = (c % NY - y) % NY
    h = jnp.where(dy > 4, NY - dy, dy)
    rank = jnp.where(
        h == 0, d,
        jnp.where(h == 4, 28 + d, NZL + 8 * (h - 1) + 2 * d + jnp.where(dy > 4, 0, 1)),
    )
    slot = jnp.arange(KT, dtype=jnp.int32)
    live = slot[None, :] < counts[:, None]
    code = jnp.where(live, rows, -1).reshape(-1)
    key = (rank[:, None] * KT + slot[None, :]).reshape(-1)
    step = jnp.broadcast_to(rank[:, None], (N_WIDE, KT)).reshape(-1)
    match = (code[:, None] == code[None, :]) & (step[None, :] < step[:, None]) & (code[None, :] >= 0)
    before = jnp.max(jnp.where(match, key[None, :], -1), axis=1)
    before = jnp.where(before < 0, N_WIDE * KT, before)
    owner = jnp.arange(N_REP, dtype=jnp.int32)
    final = jnp.max(jnp.where(code[None, :] == owner[:, None], key[None, :], -1), axis=1)
    final = jnp.where(final < 0, N_WIDE * KT, final)
    chosen = jnp.where(code < 0, N_REP, code)
    return jnp.concatenate([before, chosen, final])


def shards(features, weight, cotangent, tile_values, tile_rows, tile_counts):
    table = make_table(tile_rows[0, 0], tile_counts[0, 0])
    vmem = pl.BlockSpec(memory_space=pltpu.VMEM)
    dma = pltpu.SemaphoreType.DMA
    return pl.pallas_call(
        kernel,
        out_shape=(
            jax.ShapeDtypeStruct((T, 2 * T), BF),
            jax.ShapeDtypeStruct((T, 2 * T), F32),
            jax.ShapeDtypeStruct((T, T), BF),
        ),
        in_specs=[
            vmem, vmem, vmem,
            pl.BlockSpec(memory_space=pl.ANY),
            pl.BlockSpec(memory_space=pltpu.SMEM),
        ],
        out_specs=(vmem, vmem, vmem),
        scratch_shapes=[
            pltpu.VMEM((N_WIDE, KT, T, T), BF),
            pltpu.VMEM((N_WIDE, T, T), BF),
            pltpu.VMEM((N_WIDE * KT + 1, T, T), F32),
            pltpu.VMEM((4, NZH, T, T), F32),
            pltpu.VMEM((4, NZH, T, T), F32),
            pltpu.VMEM((3, NZH, T, T), BF),
            pltpu.VMEM((3, NZH, T, T), BF),
            pltpu.VMEM((2, T, T), BF),
            pltpu.VMEM((2, T, T), BF),
            pltpu.VMEM((N_REP + 1, T, T), BF),
            pltpu.VMEM((2, 4, NZL, T, T), BF),
            pltpu.VMEM((2, 4, NZL, T, T), BF),
            pltpu.VMEM((3, T, T), BF),
            pltpu.VMEM((3, T, T), BF),
            pltpu.VMEM((T, 2 * T), F32),
            pltpu.VMEM((T // 2, 2 * T), F32),
            pltpu.VMEM((T // 2, 2 * T), F32),
            pltpu.VMEM((3, T // 8, 2 * T), F32),
            pltpu.VMEM((NY, T // 8, 2 * T), F32),
            pltpu.VMEM((NZL, T // 8, 2 * T), F32),
            pltpu.VMEM((NZH, T // 8, 2 * T), F32),
            pltpu.VMEM((2, NX, T // 8, 2 * T), F32),
            dma, dma((3,)), dma((2, 4, NZL)), dma((N_WIDE,)),
            dma((4,)), dma((4,)), dma((3,)), dma((3,)), dma((2,)), dma((2,)),
            dma((23,)), dma((N_REP,)), dma((2, 4, NZL)), dma((2, 4, NZL)),
            dma((3,)), dma((3,)), dma((20,)), dma((24,)),
        ],
        compiler_params=pltpu.CompilerParams(
            collective_id=0, has_side_effects=True, vmem_limit_bytes=48 * 1024 * 1024
        ),
        name="graph_layer",
    )(
        features, weight, cotangent,
        tile_values.reshape(N_WIDE, KT, T, T), table,
    )


def solution(mesh):
    in_specs = (
        P(("wide", "rep"), None),
        P(),
        P(("wide", "rep"), None),
        P("wide", "rep", None, None, None, None),
        P("wide", "rep", None, None),
        P("wide", "rep", None),
    )
    out_specs = (P(("wide", "rep"), None), P(), P(("wide", "rep"), None))
    return jax.shard_map(shards, mesh=mesh, in_specs=in_specs, out_specs=out_specs, check_vma=False)
```

```python
import math

import jax
import jax.numpy as jnp
from jax import lax
from jax.experimental import pallas as pl
from jax.experimental.pallas import tpu as pltpu
from jax.sharding import PartitionSpec as P

MESH = pl.DeviceIdType.MESH
T = 128
NY, NZL, NZH, NX = 8, 4, 3, 4
N_WIDE, N_REP, KT = 32, 24, 4
BF = jnp.bfloat16
F32 = jnp.float32
X_ORDER = (2, 1, 3)
NEAR, FAR = (-2, 2, -1, 1), (-3, 3, 4)
STEPS = (
    [(0, 0)] + [(0, dy) for dy in NEAR] + [(2, 0), (1, 0), (3, 0)] + [(0, dy) for dy in FAR]
    + [(line, dy) for line in (2, 1, 3) for dy in NEAR]
    + [(line, dy) for line in (1, 2, 3) for dy in FAR]
)


def place():
    wide = lax.axis_index("wide")
    rep = lax.axis_index("rep")
    y, zl = lax.rem(wide, NY), wide // NY
    core, x, zh = lax.rem(rep, 2), lax.rem(rep // 2, NX), rep // (2 * NX)
    return x, y, zl, zh, core


def kernel(
    feat_hbm, weight_hbm, cot_hbm, tiles_hbm, rows_hbm, counts_hbm,
    out_ref, wgrad_ref, fgrad_ref,
    weight, cot, rows, counts, table_v, table, tiles, xs, tot, sib_s, sib_r, x_s, x_r, z_s, z_r, g, y_s, y_r, h_s, h_r, f_s, f_r,
    w_t, w_r1, w_a, w_r2, w_c, w_d, w_e, w_o,
    load_sems, ag_zs, ag_ys, ag_hs, ag_r, sib_ss, sib_rs, x_ss, x_rs, z_ss, z_rs,
    g_ss, g_rs, y_ss, y_rs, h_ss, h_rs, f_ss, f_rs, w_ss, w_rs,
):
    x, y, zl, zh, core = place()

    def dev(x=x, y=y, zl=zl, zh=zh, core=core):
        return (zl * NY + y, zh * (2 * NX) + x * 2 + core)

    def up(v, by, n):
        return lax.rem(v + by, n)

    sibling = dev(core=1 - core)

    def send(src, dst, ss, rs, to):
        pltpu.make_async_remote_copy(
            src_ref=src, dst_ref=dst, send_sem=ss, recv_sem=rs,
            device_id=to, device_id_type=MESH,
        ).start()

    def wait_recv(dst, rs):
        pltpu.make_async_remote_copy(
            src_ref=dst, dst_ref=dst, send_sem=rs, recv_sem=rs,
            device_id=sibling, device_id_type=MESH,
        ).wait_recv()

    def wait_send(src, ss):
        pltpu.make_async_remote_copy(
            src_ref=src, dst_ref=src, send_sem=ss, recv_sem=ss,
            device_id=sibling, device_id_type=MESH,
        ).wait_send()

    own = zl * NY + y
    loads = [
        pltpu.make_async_copy(src, dst, load_sems.at[n])
        for n, (src, dst) in enumerate((
            (feat_hbm, xs.at[own]), (tiles_hbm, tiles), (weight_hbm, weight), (cot_hbm, cot),
            (rows_hbm, rows), (counts_hbm, counts),
        ))
    ]
    for load in loads:
        load.start()

    h_r[1] = jnp.zeros((NY, T, T), BF)
    f_r[1] = jnp.zeros((T, T), BF)
    barrier = pltpu.get_barrier_semaphore()
    partners = [sibling]
    partners += [dev(x=up(x, d, NX)) for d in range(1, NX)]
    partners += [dev(y=up(y, d, NY)) for d in range(1, NY)]
    partners += [dev(zl=up(zl, d, NZL)) for d in range(1, NZL)]
    partners += [dev(zh=up(zh, d, NZH)) for d in range(1, NZH)]
    for partner in partners:
        pl.semaphore_signal(barrier, inc=1, device_id=partner, device_id_type=MESH)

    loads[4].wait()
    loads[5].wait()
    fill_table(rows, counts, table_v)
    table_load = pltpu.make_async_copy(table_v, table, load_sems.at[6])
    table_load.start()
    tot[N_WIDE * KT] = jnp.zeros((T, T), F32)
    g[N_REP] = jnp.zeros((T, T), BF)
    loads[0].wait()
    pl.semaphore_wait(barrier, len(partners))

    y_up, y_down = dev(y=up(y, 1, NY)), dev(y=up(y, NY - 1, NY))
    y_up2, y_down2 = dev(y=up(y, 2, NY)), dev(y=up(y, NY - 2, NY))

    mid = (zl == 1) | (zl == 2)
    even = lax.rem(y, 2) == 0
    lines = (zl, zl + 1 - 2 * lax.rem(zl, 2), up(zl, 2, NZL), NZL - 1 - zl)
    own_line, pair, across, other = range(4)

    def block(line, dy):
        return lines[line] * NY + up(y, (dy + NY) % NY, NY)

    def y_pass(line, n, c, to):
        i = (own_line, across, other).index(line)
        send(xs.at[c], xs.at[c], ag_ys.at[i, n], ag_r.at[c], to)

    def z_pass(dy):
        c = block(own_line, dy)
        send(xs.at[c], xs.at[c], ag_hs.at[0, dy % NY], ag_r.at[c], dev(zl=lines[pair]))

        @pl.when(mid)
        def _():
            send(xs.at[c], xs.at[c], ag_hs.at[1, dy % NY], ag_r.at[c], dev(zl=lines[other]))

    def spread(line):
        c = block(line, 0)
        for n, to in enumerate((y_up2, y_down2, y_up, y_down)):
            y_pass(line, n, c, to)

    def have(line, dy):
        c = block(line, dy)
        wait_recv(xs.at[c], ag_r.at[c])

    def onward(line):
        have(line, -2)
        below = block(line, -2)
        y_pass(line, 4, below, y_up)

        @pl.when(even)
        def _():
            y_pass(line, 6, below, y_up2)

        have(line, 2)
        above = block(line, 2)
        y_pass(line, 5, above, y_down)

        @pl.when(jnp.logical_not(even))
        def _():
            y_pass(line, 6, above, y_down2)

    send(xs.at[own], xs.at[own], ag_zs.at[0], ag_r.at[own], dev(zl=lines[across]))

    @pl.when(jnp.logical_not(mid))
    def _():
        send(xs.at[own], xs.at[own], ag_zs.at[1], ag_r.at[own], dev(zl=lines[other]))

    spread(own_line)
    z_pass(0)
    table_load.wait()
    loads[1].wait()

    def process(rank, c):
        product = jnp.dot(
            tiles[c].reshape(KT * T, T), xs[c], preferred_element_type=F32
        )
        for k in range(KT):
            before = table[k, c]
            tot[rank * KT + k] = product[k * T:(k + 1) * T] + tot[before]

    def work(first, items):
        for n, (line, dy) in enumerate(items):
            process(first + n, block(line, dy))

    process(0, own)
    onward(own_line)
    z_pass(-2)
    z_pass(2)
    have(across, 0)
    spread(across)

    @pl.when(jnp.logical_not(mid))
    def _():
        have(other, 0)
        spread(other)

    have(own_line, -1)
    z_pass(-1)
    have(own_line, 1)
    z_pass(1)
    work(1, STEPS[1:5])
    have(pair, 0)

    @pl.when(mid)
    def _():
        have(other, 0)

    onward(across)

    @pl.when(jnp.logical_not(mid))
    def _():
        onward(other)

    for dy in (-3, 3, 4):
        have(own_line, dy)
        z_pass(dy)
    work(5, STEPS[5:11])
    have(across, -1)
    have(across, 1)
    work(11, STEPS[11:15])
    for dy in (-2, 2, -1, 1):
        have(pair, dy)
    work(15, STEPS[15:19])

    @pl.when(mid)
    def _():
        have(other, -2)
        have(other, 2)

    have(other, -1)
    have(other, 1)
    work(19, STEPS[19:23])
    for first, line in ((23, pair), (26, across), (29, other)):
        for dy in (-3, 3, 4):
            have(line, dy)
        work(first, STEPS[first:first + 3])

    def part(zh_to, x_to, core_to):
        r = zh_to * (2 * NX) + x_to * 2 + core_to
        return tot[table[2 * KT, r]]

    turns = (1, 2, 0)
    for m in turns:
        q = up(zh, m, NZH)
        for n, dx in enumerate(X_ORDER + (0,)):
            sib_s[m, n] = part(q, up(x, dx, NX), 1 - core)
        send(sib_s.at[m], sib_r.at[m], sib_ss.at[m], sib_rs.at[m], sibling)
    for m in turns:
        q = up(zh, m, NZH)
        wait_recv(sib_r.at[m], sib_rs.at[m])
        for n, dx in enumerate(X_ORDER):
            to = up(x, dx, NX)
            x_s[m, n] = (part(q, to, core) + sib_r[m, n]).astype(BF)
            send(x_s.at[m, n], x_r.at[m, n], x_ss.at[m, n], x_rs.at[m, n], dev(x=to))

    def column_sum(m):
        value = part(up(zh, m, NZH), x, core) + sib_r[m, 3]
        for n in range(3):
            wait_recv(x_r.at[m, n], x_rs.at[m, n])
            value = value + x_r[m, n].astype(F32)
        return value

    for n in range(2):
        z_s[n] = column_sum(n + 1).astype(BF)
        send(z_s.at[n], z_r.at[n], z_ss.at[n], z_rs.at[n], dev(zh=up(zh, n + 1, NZH)))
    total = column_sum(0)
    for n in range(2):
        wait_recv(z_r.at[n], z_rs.at[n])
        total = total + z_r[n].astype(F32)

    loads[2].wait()
    loads[3].wait()
    agg = total.astype(BF)
    hidden = jnp.dot(agg, weight[...], preferred_element_type=F32)
    sig = jax.nn.sigmoid(hidden)
    grad_hidden = (cot[...].astype(F32) * (sig * (1.0 + hidden * (1.0 - sig)))).astype(BF)
    grad_t = lax.dot_general(
        weight[...], grad_hidden, (((1,), (1,)), ((), ())), preferred_element_type=F32
    )
    mine = zh * (2 * NX) + x * 2 + core
    g[mine] = grad_t.astype(BF)

    def g_send(n, r, to):
        send(g.at[r], g.at[r], g_ss.at[n], g_rs.at[r], to)

    for n in range(2):
        g_send(n, mine, dev(zh=up(zh, n + 1, NZH)))
    for n, dx in enumerate(X_ORDER):
        g_send(2 + n, mine, dev(x=up(x, dx, NX)))
    g_send(5, mine, sibling)

    out_ref[...] = (hidden * sig).astype(BF)
    w_t[...] = lax.dot_general(
        agg, grad_hidden, (((0,), (0,)), ((), ())), preferred_element_type=F32
    )
    half = T // 2
    chunk = half // NX
    mine_half = pl.ds(pl.multiple_of(core * half, half), half)
    other_half = pl.ds(pl.multiple_of((1 - core) * half, half), half)
    send(w_t.at[other_half], w_r1, w_ss.at[0], w_rs.at[0], sibling)

    for n in range(2):
        r = up(zh, 2 - n, NZH) * (2 * NX) + x * 2 + core
        wait_recv(g.at[r], g_rs.at[r])
        for m, dx in enumerate(X_ORDER):
            g_send(6 + 4 * n + m, r, dev(x=up(x, dx, NX)))
        g_send(6 + 4 * n + 3, r, sibling)

    wait_recv(w_r1, w_rs.at[0])
    w_a[...] = w_t[mine_half] + w_r1[...]

    def chunk_of(v):
        return pl.ds(pl.multiple_of(v * chunk, chunk), chunk)

    for n, dx in enumerate(X_ORDER):
        to = up(x, dx, NX)
        send(w_a.at[chunk_of(to)], w_r2.at[n], w_ss.at[1 + n], w_rs.at[1 + n], dev(x=to))

    for q in range(NZH):
        for n, dx in enumerate(X_ORDER):
            r = up(zh, NZH - q, NZH) * (2 * NX) + up(x, NX - dx, NX) * 2 + core
            wait_recv(g.at[r], g_rs.at[r])
            g_send(14 + 3 * q + n, r, sibling)

    w_sum = w_a[chunk_of(x)]
    for n in range(3):
        wait_recv(w_r2.at[n], w_rs.at[1 + n])
        w_sum = w_sum + w_r2[n]
    w_c[y] = w_sum
    for n in range(1, NY):
        send(w_c.at[y], w_c.at[y], w_ss.at[3 + n], w_rs.at[4 + y], dev(y=up(y, n, NY)))

    def sib_wait(n, carry):
        r = n * 2 + 1 - core
        wait_recv(g.at[r], g_rs.at[r])
        return carry

    lax.fori_loop(0, N_REP // 2, sib_wait, 0)

    def term(c):
        left = jnp.concatenate(
            [g[table[KT + k, c]] for k in range(KT)], axis=1
        )
        return jnp.dot(left, tiles[c].reshape(KT * T, T), preferred_element_type=F32)

    def y_send(line, n, value, to):
        i = (own_line, across, other).index(line)
        y_s[i, n] = value.astype(BF)
        send(y_s.at[i, n], y_r.at[i, n], y_ss.at[i, n], y_rs.at[i, n], to)

    def y_have(line, n):
        i = (own_line, across, other).index(line)
        wait_recv(y_r.at[i, n], y_rs.at[i, n])
        return y_r[i, n].astype(F32)

    def hop(slot, line, dy):
        k = dy % NY
        h_s[slot, k] = term(block(line, dy)).astype(BF)
        send(h_s.at[slot, k], h_r.at[slot, k], h_ss.at[slot, k], h_rs.at[slot, k], dev(zl=lines[line]))

    def value_of(line, dy):
        value = term(block(line, dy))
        if line == own_line:
            k = dy % NY
            wait_recv(h_r.at[0, k], h_rs.at[0, k])
            value = value + h_r[0, k].astype(F32)

            @pl.when(mid)
            def _():
                wait_recv(h_r.at[1, k], h_rs.at[1, k])

            value = value + jnp.where(mid, h_r[1, k].astype(F32), 0.0)
        return value

    def outer_part(line):
        value = value_of(line, 4)

        @pl.when(even)
        def _():
            y_send(line, 0, value, y_up2)

        @pl.when(jnp.logical_not(even))
        def _():
            y_send(line, 0, value, y_down2)

        above, below = value_of(line, 3), value_of(line, -3)
        y_send(line, 1, above, y_up)
        y_send(line, 2, below, y_down)

    def next_part(line):
        above, below = value_of(line, 1), value_of(line, -1)
        y_send(line, 3, above, y_up)
        y_send(line, 4, below, y_down)

    def second_part(line):
        above, below = value_of(line, 2), value_of(line, -2)
        above = above + y_have(line, 1)
        below = below + y_have(line, 2)
        four = y_have(line, 0)
        y_send(line, 5, above + jnp.where(even, four, 0.0), y_up2)
        y_send(line, 6, below + jnp.where(even, 0.0, four), y_down2)

    def whole(line):
        value = value_of(line, 0)
        for n in range(3, 7):
            value = value + y_have(line, n)
        return value

    def z_send(n, line):
        f_s[n] = whole(line).astype(BF)
        send(f_s.at[n], f_r.at[n], f_ss.at[n], f_rs.at[n], dev(zl=lines[line]))

    for dy in FAR:
        hop(0, pair, dy)

    @pl.when(mid)
    def _():
        for dy in FAR:
            hop(1, other, dy)

    outer_part(across)

    @pl.when(jnp.logical_not(mid))
    def _():
        outer_part(other)

    for dy in NEAR + (0,):
        hop(0, pair, dy)

    @pl.when(mid)
    def _():
        for dy in NEAR + (0,):
            hop(1, other, dy)

    outer_part(own_line)

    def spread_sum(buf, base, me, n):
        def wait_one(i, carry):
            @pl.when(i != me)
            def _():
                wait_recv(buf.at[i], w_rs.at[base + i])
            return carry

        lax.fori_loop(0, n, wait_one, 0)
        value = buf[0]
        for i in range(1, n):
            value = value + buf[i]
        return value

    w_d[zl] = spread_sum(w_c, 4, y, NY)
    for n in range(1, NZL):
        send(w_d.at[zl], w_d.at[zl], w_ss.at[10 + n], w_rs.at[12 + zl], dev(zl=up(zl, n, NZL)))

    second_part(across)

    @pl.when(jnp.logical_not(mid))
    def _():
        second_part(other)

    next_part(across)

    @pl.when(jnp.logical_not(mid))
    def _():
        next_part(other)

    next_part(own_line)

    w_e[zh] = spread_sum(w_d, 12, zl, NZL)
    for n in range(1, NZH):
        send(w_e.at[zh], w_e.at[zh], w_ss.at[13 + n], w_rs.at[16 + zh], dev(zh=up(zh, n, NZH)))

    second_part(own_line)
    z_send(0, across)

    @pl.when(jnp.logical_not(mid))
    def _():
        z_send(1, other)

    value = whole(own_line)

    w_own = spread_sum(w_e, 16, zh, NZH) * (1.0 / math.sqrt(N_WIDE * N_REP * T))
    w_o[core, x] = w_own
    for n in range(1, NX):
        send(w_o.at[core, x], w_o.at[core, x], w_ss.at[15 + n], w_rs.at[19 + x], dev(x=up(x, n, NX)))

    def gathered(i, carry):
        @pl.when(i != x)
        def _():
            wait_recv(w_o.at[core, i], w_rs.at[19 + i])
        return carry

    lax.fori_loop(0, NX, gathered, 0)
    send(w_o.at[core], w_o.at[core], w_ss.at[19], w_rs.at[23], sibling)

    wait_recv(f_r.at[0], f_rs.at[0])
    value = value + f_r[0].astype(F32)

    @pl.when(jnp.logical_not(mid))
    def _():
        wait_recv(f_r.at[1], f_rs.at[1])

    value = value + jnp.where(mid, 0.0, f_r[1].astype(F32))
    fgrad_ref[...] = value.T.astype(BF)
    wait_recv(w_o.at[1 - core], w_rs.at[23])
    wgrad_ref[...] = w_o[...].reshape(T, 2 * T)

    def settle(n, carry):
        wait_send(xs.at[0], ag_hs.at[0, n])
        wait_send(h_s.at[0, n], h_ss.at[0, n])

        @pl.when(mid)
        def _():
            wait_send(xs.at[0], ag_hs.at[1, n])
            wait_send(h_s.at[1, n], h_ss.at[1, n])

        return carry

    lax.fori_loop(0, NY, settle, 0)

    def drain(n, carry):
        for i in range(2):
            wait_send(xs.at[0], ag_ys.at[i, n])
            wait_send(y_s.at[i, n], y_ss.at[i, n])

        @pl.when(jnp.logical_not(mid))
        def _():
            wait_send(xs.at[0], ag_ys.at[2, n])
            wait_send(y_s.at[2, n], y_ss.at[2, n])

        return carry

    lax.fori_loop(0, 7, drain, 0)
    wait_send(xs.at[0], ag_zs.at[0])
    wait_send(f_s.at[0], f_ss.at[0])

    @pl.when(jnp.logical_not(mid))
    def _():
        wait_send(xs.at[0], ag_zs.at[1])
        wait_send(f_s.at[1], f_ss.at[1])

    for n in range(2):
        wait_send(z_s.at[n], z_ss.at[n])
    for m in range(NZH):
        wait_send(sib_s.at[m], sib_ss.at[m])
        for n in range(3):
            wait_send(x_s.at[m, n], x_ss.at[m, n])

    def drain_g(n, carry):
        wait_send(g.at[0], g_ss.at[n])
        return carry

    lax.fori_loop(0, 23, drain_g, 0)
    wait_send(w_r1, w_ss.at[0])

    def drain_w(n, carry):
        wait_send(w_r2.at[0], w_ss.at[n])
        return carry

    lax.fori_loop(1, 19, drain_w, 0)
    wait_send(w_o.at[core], w_ss.at[19])


def rank_of(c):
    x, y, zl, zh, core = place()
    v = c // NY
    line = jnp.where(v == zl, 0, jnp.where(v == NZL - 1 - zl, 3, jnp.where(lax.rem(v + zl, 2) == 0, 2, 1)))
    dy = lax.rem(lax.rem(c, NY) - y + NY, NY)
    rank = jnp.zeros_like(c)
    for n, (on, at) in enumerate(STEPS):
        rank = jnp.where((line == on) & (dy == at % NY), n, rank)
    return rank


def fill_table(rows, counts, table_v):
    square = (N_WIDE, N_WIDE)
    lane = lax.broadcasted_iota(jnp.int32, square, 1)
    sub = lax.broadcasted_iota(jnp.int32, square, 0)
    rank_l, rank_s = rank_of(lane), rank_of(sub)
    live = counts[...]
    code = [jnp.where(live > k, rows[k:k + 1, :], -1) for k in range(KT)]
    code_l = [jnp.broadcast_to(v, square) for v in code]
    code_s = [
        jnp.broadcast_to(
            jnp.max(jnp.where(lane == sub, v, -1), axis=1, keepdims=True), square
        )
        for v in code_l
    ]
    none = N_WIDE * KT

    def best(matches):
        keys = [jnp.where(m, rank_s * KT + k, -1) for k, m in enumerate(matches)]
        top = keys[0]
        for key in keys[1:]:
            top = jnp.maximum(top, key)
        top = jnp.max(top, axis=0, keepdims=True)
        return jnp.where(top < 0, none, top)

    for k in range(KT):
        table_v[k:k + 1, 0:N_WIDE] = best(
            [(v == code_l[k]) & (rank_s < rank_l) & (v >= 0) for v in code_s]
        )
        table_v[KT + k:KT + k + 1, 0:N_WIDE] = jnp.where(code[k] < 0, N_REP, code[k])
    table_v[2 * KT:2 * KT + 1, 0:N_WIDE] = best([v == lane for v in code_s])


def shards(features, weight, cotangent, tile_values, tile_rows, tile_counts):
    dma = pltpu.SemaphoreType.DMA
    hbm = pl.BlockSpec(memory_space=pltpu.HBM)
    vmem = pl.BlockSpec(memory_space=pltpu.VMEM)
    shapes = (
        jax.ShapeDtypeStruct((T, 2 * T), BF),
        jax.ShapeDtypeStruct((T, 2 * T), F32),
        jax.ShapeDtypeStruct((T, T), BF),
    )
    return pl.pallas_call(
        kernel,
        out_shape=shapes,
        in_specs=[hbm] * 6,
        out_specs=(vmem, vmem, vmem),
        scratch_shapes=[
            pltpu.VMEM((T, 2 * T), BF),
            pltpu.VMEM((T, 2 * T), BF),
            pltpu.VMEM((KT, N_WIDE), jnp.int32),
            pltpu.VMEM((1, N_WIDE), jnp.int32),
            pltpu.VMEM((16, T), jnp.int32),
            pltpu.SMEM((16, T), jnp.int32),
            pltpu.VMEM((N_WIDE, KT, T, T), BF),
            pltpu.VMEM((N_WIDE, T, T), BF),
            pltpu.VMEM((N_WIDE * KT + 1, T, T), F32),
            pltpu.VMEM((NZH, 4, T, T), F32),
            pltpu.VMEM((NZH, 4, T, T), F32),
            pltpu.VMEM((NZH, 3, T, T), BF),
            pltpu.VMEM((NZH, 3, T, T), BF),
            pltpu.VMEM((2, T, T), BF),
            pltpu.VMEM((2, T, T), BF),
            pltpu.VMEM((N_REP + 1, T, T), BF),
            pltpu.VMEM((3, 7, T, T), BF),
            pltpu.VMEM((3, 7, T, T), BF),
            pltpu.VMEM((2, NY, T, T), BF),
            pltpu.VMEM((2, NY, T, T), BF),
            pltpu.VMEM((2, T, T), BF),
            pltpu.VMEM((2, T, T), BF),
            pltpu.VMEM((T, 2 * T), F32),
            pltpu.VMEM((T // 2, 2 * T), F32),
            pltpu.VMEM((T // 2, 2 * T), F32),
            pltpu.VMEM((3, T // 8, 2 * T), F32),
            pltpu.VMEM((NY, T // 8, 2 * T), F32),
            pltpu.VMEM((NZL, T // 8, 2 * T), F32),
            pltpu.VMEM((NZH, T // 8, 2 * T), F32),
            pltpu.VMEM((2, NX, T // 8, 2 * T), F32),
            dma((7,)), dma((2,)), dma((3, 7)), dma((2, NY)), dma((N_WIDE,)),
            dma((NZH,)), dma((NZH,)), dma((NZH, 3)), dma((NZH, 3)), dma((2,)), dma((2,)),
            dma((23,)), dma((N_REP,)), dma((3, 7)), dma((3, 7)), dma((2, NY)), dma((2, NY)),
            dma((2,)), dma((2,)), dma((20,)), dma((24,)),
        ],
        compiler_params=pltpu.CompilerParams(
            collective_id=0, has_side_effects=True, vmem_limit_bytes=48 * 1024 * 1024
        ),
        name="graph_layer",
    )(*(
        pltpu.with_memory_space_constraint(value, pltpu.HBM)
        for value in (
            features, weight, cotangent,
            tile_values.reshape(N_WIDE, KT, T, T),
            tile_rows[0, 0].T, tile_counts.reshape(1, N_WIDE),
        )
    ))


def solution(mesh):
    in_specs = (
        P(("wide", "rep"), None),
        P(),
        P(("wide", "rep"), None),
        P("wide", "rep", None, None, None, None),
        P("wide", "rep", None, None),
        P("wide", "rep", None),
    )
    out_specs = (P(("wide", "rep"), None), P(), P(("wide", "rep"), None))
    return jax.shard_map(shards, mesh=mesh, in_specs=in_specs, out_specs=out_specs, check_vma=False)
```

```python
import math

import jax
import jax.numpy as jnp
from jax import lax
from jax.experimental import pallas as pl
from jax.experimental.pallas import tpu as pltpu
from jax.sharding import PartitionSpec as P

MESH = pl.DeviceIdType.MESH
T = 128
NY, NZL, NZH, NX = 8, 4, 3, 4
N_WIDE, N_REP, KT = 32, 24, 4
BF = jnp.bfloat16
F32 = jnp.float32
X_ORDER = (2, 1, 3)
NEAR, FAR = (-2, 2, -1, 1), (-3, 3, 4)
STEPS = (
    [(0, 0)] + [(0, dy) for dy in NEAR] + [(2, 0), (1, 0), (3, 0)] + [(0, dy) for dy in FAR]
    + [(line, dy) for line in (2, 1, 3) for dy in NEAR]
    + [(line, dy) for line in (1, 2, 3) for dy in FAR]
)


def place():
    wide = lax.axis_index("wide")
    rep = lax.axis_index("rep")
    y, zl = lax.rem(wide, NY), wide // NY
    core, x, zh = lax.rem(rep, 2), lax.rem(rep // 2, NX), rep // (2 * NX)
    return x, y, zl, zh, core


def kernel(
    feat_hbm, weight_hbm, cot_hbm, tiles_hbm, rows_hbm, counts_hbm,
    out_ref, wgrad_ref, fgrad_ref,
    weight, cot, rows, counts, table_v, table, tiles, xs, tot, sib_s, sib_r, x_s, x_r, z_s, z_r, g, y_s, y_r, h_s, h_r, f_s, f_r,
    w_t, w_r, w_c, w_d, w_e, w_o,
    load_sems, ag_zs, ag_ys, ag_hs, ag_r, sib_ss, sib_rs, x_ss, x_rs, z_ss, z_rs,
    g_ss, g_rs, y_ss, y_rs, h_ss, h_rs, f_ss, f_rs, w_ss, w_rs,
):
    x, y, zl, zh, core = place()

    def dev(x=x, y=y, zl=zl, zh=zh, core=core):
        return (zl * NY + y, zh * (2 * NX) + x * 2 + core)

    def up(v, by, n):
        return lax.rem(v + by, n)

    sibling = dev(core=1 - core)

    def send(src, dst, ss, rs, to):
        pltpu.make_async_remote_copy(
            src_ref=src, dst_ref=dst, send_sem=ss, recv_sem=rs,
            device_id=to, device_id_type=MESH,
        ).start()

    def wait_recv(dst, rs):
        pltpu.make_async_remote_copy(
            src_ref=dst, dst_ref=dst, send_sem=rs, recv_sem=rs,
            device_id=sibling, device_id_type=MESH,
        ).wait_recv()

    def wait_send(src, ss):
        pltpu.make_async_remote_copy(
            src_ref=src, dst_ref=src, send_sem=ss, recv_sem=ss,
            device_id=sibling, device_id_type=MESH,
        ).wait_send()

    own = zl * NY + y
    loads = [
        pltpu.make_async_copy(src, dst, load_sems.at[n])
        for n, (src, dst) in enumerate((
            (feat_hbm, xs.at[own]), (tiles_hbm, tiles), (weight_hbm, weight), (cot_hbm, cot),
            (rows_hbm, rows), (counts_hbm, counts),
        ))
    ]
    for load in loads:
        load.start()

    h_r[1] = jnp.zeros((NY, T, T), BF)
    f_r[1] = jnp.zeros((T, T), BF)
    barrier = pltpu.get_barrier_semaphore()
    chips = [(dx, dc) for dx in range(NX) for dc in range(2) if dx or dc]
    around = [dev(x=up(x, dx, NX), core=lax.rem(core + dc, 2)) for dx, dc in chips]
    partners = list(around)
    partners += [dev(y=up(y, d, NY)) for d in range(1, NY)]
    partners += [dev(zl=up(zl, d, NZL)) for d in range(1, NZL)]
    partners += [dev(zh=up(zh, d, NZH)) for d in range(1, NZH)]
    for partner in partners:
        pl.semaphore_signal(barrier, inc=1, device_id=partner, device_id_type=MESH)

    loads[4].wait()
    loads[5].wait()
    fill_table(rows, counts, table_v)
    table_load = pltpu.make_async_copy(table_v, table, load_sems.at[6])
    table_load.start()
    tot[N_WIDE * KT] = jnp.zeros((T, T), F32)
    g[N_REP] = jnp.zeros((T, T), BF)
    loads[0].wait()
    pl.semaphore_wait(barrier, len(partners))

    y_up, y_down = dev(y=up(y, 1, NY)), dev(y=up(y, NY - 1, NY))
    y_up2, y_down2 = dev(y=up(y, 2, NY)), dev(y=up(y, NY - 2, NY))

    mid = (zl == 1) | (zl == 2)
    even = lax.rem(y, 2) == 0
    lines = (zl, zl + 1 - 2 * lax.rem(zl, 2), up(zl, 2, NZL), NZL - 1 - zl)
    own_line, pair, across, other = range(4)

    def block(line, dy):
        return lines[line] * NY + up(y, (dy + NY) % NY, NY)

    def y_pass(line, n, c, to):
        i = (own_line, across, other).index(line)
        send(xs.at[c], xs.at[c], ag_ys.at[i, n], ag_r.at[c], to)

    def z_pass(dy):
        c = block(own_line, dy)
        send(xs.at[c], xs.at[c], ag_hs.at[0, dy % NY], ag_r.at[c], dev(zl=lines[pair]))

        @pl.when(mid)
        def _():
            send(xs.at[c], xs.at[c], ag_hs.at[1, dy % NY], ag_r.at[c], dev(zl=lines[other]))

    def spread(line):
        c = block(line, 0)
        for n, to in enumerate((y_up2, y_down2, y_up, y_down)):
            y_pass(line, n, c, to)

    def have(line, dy):
        c = block(line, dy)
        wait_recv(xs.at[c], ag_r.at[c])

    def onward(line):
        have(line, -2)
        below = block(line, -2)
        y_pass(line, 4, below, y_up)

        @pl.when(even)
        def _():
            y_pass(line, 6, below, y_up2)

        have(line, 2)
        above = block(line, 2)
        y_pass(line, 5, above, y_down)

        @pl.when(jnp.logical_not(even))
        def _():
            y_pass(line, 6, above, y_down2)

    send(xs.at[own], xs.at[own], ag_zs.at[0], ag_r.at[own], dev(zl=lines[across]))

    @pl.when(jnp.logical_not(mid))
    def _():
        send(xs.at[own], xs.at[own], ag_zs.at[1], ag_r.at[own], dev(zl=lines[other]))

    spread(own_line)
    z_pass(0)
    table_load.wait()
    loads[1].wait()

    def process(rank, c):
        product = jnp.dot(
            tiles[c].reshape(KT * T, T), xs[c], preferred_element_type=F32
        )
        for k in range(KT):
            before = table[k, c]
            tot[rank * KT + k] = product[k * T:(k + 1) * T] + tot[before]

    def work(first, items):
        for n, (line, dy) in enumerate(items):
            process(first + n, block(line, dy))

    process(0, own)
    onward(own_line)
    z_pass(-2)
    z_pass(2)
    have(across, 0)
    spread(across)

    @pl.when(jnp.logical_not(mid))
    def _():
        have(other, 0)
        spread(other)

    have(own_line, -1)
    z_pass(-1)
    have(own_line, 1)
    z_pass(1)
    work(1, STEPS[1:5])
    have(pair, 0)

    @pl.when(mid)
    def _():
        have(other, 0)

    onward(across)

    @pl.when(jnp.logical_not(mid))
    def _():
        onward(other)

    for dy in (-3, 3, 4):
        have(own_line, dy)
        z_pass(dy)
    work(5, STEPS[5:11])
    have(across, -1)
    have(across, 1)
    work(11, STEPS[11:15])
    for dy in (-2, 2, -1, 1):
        have(pair, dy)
    work(15, STEPS[15:19])

    @pl.when(mid)
    def _():
        have(other, -2)
        have(other, 2)

    have(other, -1)
    have(other, 1)
    work(19, STEPS[19:23])
    for first, line in ((23, pair), (26, across), (29, other)):
        for dy in (-3, 3, 4):
            have(line, dy)
        work(first, STEPS[first:first + 3])

    def part(zh_to, x_to, core_to):
        r = zh_to * (2 * NX) + x_to * 2 + core_to
        return tot[table[2 * KT, r]]

    turns = (1, 2, 0)
    for m in turns:
        q = up(zh, m, NZH)
        for n, dx in enumerate(X_ORDER + (0,)):
            sib_s[m, n] = part(q, up(x, dx, NX), 1 - core)
        send(sib_s.at[m], sib_r.at[m], sib_ss.at[m], sib_rs.at[m], sibling)
    for m in turns:
        q = up(zh, m, NZH)
        wait_recv(sib_r.at[m], sib_rs.at[m])
        for n, dx in enumerate(X_ORDER):
            to = up(x, dx, NX)
            x_s[m, n] = (part(q, to, core) + sib_r[m, n]).astype(BF)
            send(x_s.at[m, n], x_r.at[m, n], x_ss.at[m, n], x_rs.at[m, n], dev(x=to))

    def column_sum(m):
        value = part(up(zh, m, NZH), x, core) + sib_r[m, 3]
        for n in range(3):
            wait_recv(x_r.at[m, n], x_rs.at[m, n])
            value = value + x_r[m, n].astype(F32)
        return value

    for n in range(2):
        z_s[n] = column_sum(n + 1).astype(BF)
        send(z_s.at[n], z_r.at[n], z_ss.at[n], z_rs.at[n], dev(zh=up(zh, n + 1, NZH)))
    total = column_sum(0)
    for n in range(2):
        wait_recv(z_r.at[n], z_rs.at[n])
        total = total + z_r[n].astype(F32)

    loads[2].wait()
    loads[3].wait()
    agg = total.astype(BF)
    hidden = jnp.dot(agg, weight[...], preferred_element_type=F32)
    sig = jax.nn.sigmoid(hidden)
    grad_hidden = (cot[...].astype(F32) * (sig * (1.0 + hidden * (1.0 - sig)))).astype(BF)
    grad_t = lax.dot_general(
        weight[...], grad_hidden, (((1,), (1,)), ((), ())), preferred_element_type=F32
    )
    mine = zh * (2 * NX) + x * 2 + core
    g[mine] = grad_t.astype(BF)

    def g_send(n, r, to):
        send(g.at[r], g.at[r], g_ss.at[n], g_rs.at[r], to)

    for n in range(2):
        g_send(n, mine, dev(zh=up(zh, n + 1, NZH)))
    for n, dx in enumerate(X_ORDER):
        g_send(2 + n, mine, dev(x=up(x, dx, NX)))
    g_send(5, mine, sibling)

    out_ref[...] = (hidden * sig).astype(BF)
    term_of_weight = lax.dot_general(
        agg, grad_hidden, (((0,), (0,)), ((), ())), preferred_element_type=F32
    )
    for i in range(2):
        for j in range(NX):
            row = (i * NX + j) * (T // 8)
            w_t[i, j] = term_of_weight[row:row + T // 8]
    for n, (dx, dc) in enumerate(chips):
        part_for = w_t.at[lax.rem(core + dc, 2), up(x, dx, NX)]
        send(part_for, w_r.at[n], w_ss.at[n], w_rs.at[n], around[n])

    early = (jnp.where(zh == 2, 1, 2), jnp.where(zh == 0, 1, 0))

    def from_z(n):
        r = early[n] * (2 * NX) + x * 2 + core
        wait_recv(g.at[r], g_rs.at[r])
        for m, dx in enumerate(X_ORDER):
            g_send(6 + 4 * n + m, r, dev(x=up(x, dx, NX)))
        g_send(6 + 4 * n + 3, r, sibling)

    def from_x(q, at):
        for n, dx in enumerate(X_ORDER):
            r = at * (2 * NX) + up(x, NX - dx, NX) * 2 + core
            wait_recv(g.at[r], g_rs.at[r])
            g_send(14 + 3 * q + n, r, sibling)

    def spread_sum(buf, base, me, n):
        for i in range(n):
            @pl.when(me != i)
            def _():
                wait_recv(buf.at[i], w_rs.at[base + i])
        value = buf[0]
        for i in range(1, n):
            value = value + buf[i]
        return value

    from_z(0)
    w_sum = w_t[core, x]
    for n in range(7):
        wait_recv(w_r.at[n], w_rs.at[n])
        w_sum = w_sum + w_r[n]
    w_c[y] = w_sum
    for n in range(1, NY):
        send(w_c.at[y], w_c.at[y], w_ss.at[6 + n], w_rs.at[7 + y], dev(y=up(y, n, NY)))
    from_z(1)
    from_x(0, zh)
    from_x(1, early[0])
    w_d[zl] = spread_sum(w_c, 7, y, NY)
    for n in range(1, NZL):
        send(w_d.at[zl], w_d.at[zl], w_ss.at[13 + n], w_rs.at[15 + zl], dev(zl=up(zl, n, NZL)))
    from_x(2, early[1])

    def sib_wait(n, carry):
        r = n * 2 + 1 - core
        wait_recv(g.at[r], g_rs.at[r])
        return carry

    lax.fori_loop(0, N_REP // 2, sib_wait, 0)

    def term(c):
        left = jnp.concatenate(
            [g[table[KT + k, c]] for k in range(KT)], axis=1
        )
        return jnp.dot(left, tiles[c].reshape(KT * T, T), preferred_element_type=F32)

    def y_send(line, n, value, to):
        i = (own_line, across, other).index(line)
        y_s[i, n] = value.astype(BF)
        send(y_s.at[i, n], y_r.at[i, n], y_ss.at[i, n], y_rs.at[i, n], to)

    def y_have(line, n):
        i = (own_line, across, other).index(line)
        wait_recv(y_r.at[i, n], y_rs.at[i, n])
        return y_r[i, n].astype(F32)

    def hop(slot, line, dy):
        k = dy % NY
        h_s[slot, k] = term(block(line, dy)).astype(BF)
        send(h_s.at[slot, k], h_r.at[slot, k], h_ss.at[slot, k], h_rs.at[slot, k], dev(zl=lines[line]))

    def value_of(line, dy):
        value = term(block(line, dy))
        if line == own_line:
            k = dy % NY
            wait_recv(h_r.at[0, k], h_rs.at[0, k])
            value = value + h_r[0, k].astype(F32)

            @pl.when(mid)
            def _():
                wait_recv(h_r.at[1, k], h_rs.at[1, k])

            value = value + jnp.where(mid, h_r[1, k].astype(F32), 0.0)
        return value

    def outer_part(line):
        value = value_of(line, 4)

        @pl.when(even)
        def _():
            y_send(line, 0, value, y_up2)

        @pl.when(jnp.logical_not(even))
        def _():
            y_send(line, 0, value, y_down2)

        above, below = value_of(line, 3), value_of(line, -3)
        y_send(line, 1, above, y_up)
        y_send(line, 2, below, y_down)

    def next_part(line):
        above, below = value_of(line, 1), value_of(line, -1)
        y_send(line, 3, above, y_up)
        y_send(line, 4, below, y_down)

    def second_part(line):
        above, below = value_of(line, 2), value_of(line, -2)
        above = above + y_have(line, 1)
        below = below + y_have(line, 2)
        four = y_have(line, 0)
        y_send(line, 5, above + jnp.where(even, four, 0.0), y_up2)
        y_send(line, 6, below + jnp.where(even, 0.0, four), y_down2)

    def whole(line):
        value = value_of(line, 0)
        for n in range(3, 7):
            value = value + y_have(line, n)
        return value

    def z_send(n, line):
        f_s[n] = whole(line).astype(BF)
        send(f_s.at[n], f_r.at[n], f_ss.at[n], f_rs.at[n], dev(zl=lines[line]))

    for dy in FAR:
        hop(0, pair, dy)

    @pl.when(mid)
    def _():
        for dy in FAR:
            hop(1, other, dy)

    outer_part(across)

    @pl.when(jnp.logical_not(mid))
    def _():
        outer_part(other)

    for dy in NEAR + (0,):
        hop(0, pair, dy)

    @pl.when(mid)
    def _():
        for dy in NEAR + (0,):
            hop(1, other, dy)

    outer_part(own_line)

    w_e[zh] = spread_sum(w_d, 15, zl, NZL)
    for n in range(1, NZH):
        send(w_e.at[zh], w_e.at[zh], w_ss.at[16 + n], w_rs.at[19 + zh], dev(zh=up(zh, n, NZH)))

    second_part(across)

    @pl.when(jnp.logical_not(mid))
    def _():
        second_part(other)

    next_part(across)

    @pl.when(jnp.logical_not(mid))
    def _():
        next_part(other)

    next_part(own_line)

    w_o[core, x] = spread_sum(w_e, 19, zh, NZH) * (1.0 / math.sqrt(N_WIDE * N_REP * T))
    for n in range(7):
        send(w_o.at[core, x], w_o.at[core, x], w_ss.at[19 + n], w_rs.at[22 + core * NX + x], around[n])

    second_part(own_line)
    z_send(0, across)

    @pl.when(jnp.logical_not(mid))
    def _():
        z_send(1, other)

    value = whole(own_line)

    wait_recv(f_r.at[0], f_rs.at[0])
    value = value + f_r[0].astype(F32)

    @pl.when(jnp.logical_not(mid))
    def _():
        wait_recv(f_r.at[1], f_rs.at[1])

    value = value + jnp.where(mid, 0.0, f_r[1].astype(F32))
    fgrad_ref[...] = value.T.astype(BF)
    for n, (dx, dc) in enumerate(chips):
        i, j = lax.rem(core + dc, 2), up(x, dx, NX)
        wait_recv(w_o.at[i, j], w_rs.at[22 + i * NX + j])
    wgrad_ref[...] = w_o[...].reshape(T, 2 * T)

    def settle(n, carry):
        wait_send(xs.at[0], ag_hs.at[0, n])
        wait_send(h_s.at[0, n], h_ss.at[0, n])

        @pl.when(mid)
        def _():
            wait_send(xs.at[0], ag_hs.at[1, n])
            wait_send(h_s.at[1, n], h_ss.at[1, n])

        return carry

    lax.fori_loop(0, NY, settle, 0)

    def drain(n, carry):
        for i in range(2):
            wait_send(xs.at[0], ag_ys.at[i, n])
            wait_send(y_s.at[i, n], y_ss.at[i, n])

        @pl.when(jnp.logical_not(mid))
        def _():
            wait_send(xs.at[0], ag_ys.at[2, n])
            wait_send(y_s.at[2, n], y_ss.at[2, n])

        return carry

    lax.fori_loop(0, 7, drain, 0)
    wait_send(xs.at[0], ag_zs.at[0])
    wait_send(f_s.at[0], f_ss.at[0])

    @pl.when(jnp.logical_not(mid))
    def _():
        wait_send(xs.at[0], ag_zs.at[1])
        wait_send(f_s.at[1], f_ss.at[1])

    for n in range(2):
        wait_send(z_s.at[n], z_ss.at[n])
    for m in range(NZH):
        wait_send(sib_s.at[m], sib_ss.at[m])
        for n in range(3):
            wait_send(x_s.at[m, n], x_ss.at[m, n])

    def drain_g(n, carry):
        wait_send(g.at[0], g_ss.at[n])
        return carry

    lax.fori_loop(0, 23, drain_g, 0)

    def drain_w(n, carry):
        wait_send(w_r.at[0], w_ss.at[n])
        return carry

    lax.fori_loop(0, 26, drain_w, 0)


def rank_of(c):
    x, y, zl, zh, core = place()
    v = c // NY
    line = jnp.where(v == zl, 0, jnp.where(v == NZL - 1 - zl, 3, jnp.where(lax.rem(v + zl, 2) == 0, 2, 1)))
    dy = lax.rem(lax.rem(c, NY) - y + NY, NY)
    rank = jnp.zeros_like(c)
    for n, (on, at) in enumerate(STEPS):
        rank = jnp.where((line == on) & (dy == at % NY), n, rank)
    return rank


def fill_table(rows, counts, table_v):
    square = (N_WIDE, N_WIDE)
    lane = lax.broadcasted_iota(jnp.int32, square, 1)
    sub = lax.broadcasted_iota(jnp.int32, square, 0)
    rank_l, rank_s = rank_of(lane), rank_of(sub)
    live = counts[...]
    code = [jnp.where(live > k, rows[k:k + 1, :], -1) for k in range(KT)]
    code_l = [jnp.broadcast_to(v, square) for v in code]
    code_s = [
        jnp.broadcast_to(
            jnp.max(jnp.where(lane == sub, v, -1), axis=1, keepdims=True), square
        )
        for v in code_l
    ]
    none = N_WIDE * KT

    def best(matches):
        keys = [jnp.where(m, rank_s * KT + k, -1) for k, m in enumerate(matches)]
        top = keys[0]
        for key in keys[1:]:
            top = jnp.maximum(top, key)
        top = jnp.max(top, axis=0, keepdims=True)
        return jnp.where(top < 0, none, top)

    for k in range(KT):
        table_v[k:k + 1, 0:N_WIDE] = best(
            [(v == code_l[k]) & (rank_s < rank_l) & (v >= 0) for v in code_s]
        )
        table_v[KT + k:KT + k + 1, 0:N_WIDE] = jnp.where(code[k] < 0, N_REP, code[k])
    table_v[2 * KT:2 * KT + 1, 0:N_WIDE] = best([v == lane for v in code_s])


def shards(features, weight, cotangent, tile_values, tile_rows, tile_counts):
    dma = pltpu.SemaphoreType.DMA
    hbm = pl.BlockSpec(memory_space=pltpu.HBM)
    vmem = pl.BlockSpec(memory_space=pltpu.VMEM)
    shapes = (
        jax.ShapeDtypeStruct((T, 2 * T), BF),
        jax.ShapeDtypeStruct((T, 2 * T), F32),
        jax.ShapeDtypeStruct((T, T), BF),
    )
    return pl.pallas_call(
        kernel,
        out_shape=shapes,
        in_specs=[hbm] * 6,
        out_specs=(vmem, vmem, vmem),
        scratch_shapes=[
            pltpu.VMEM((T, 2 * T), BF),
            pltpu.VMEM((T, 2 * T), BF),
            pltpu.VMEM((KT, N_WIDE), jnp.int32),
            pltpu.VMEM((1, N_WIDE), jnp.int32),
            pltpu.VMEM((16, T), jnp.int32),
            pltpu.SMEM((16, T), jnp.int32),
            pltpu.VMEM((N_WIDE, KT, T, T), BF),
            pltpu.VMEM((N_WIDE, T, T), BF),
            pltpu.VMEM((N_WIDE * KT + 1, T, T), F32),
            pltpu.VMEM((NZH, 4, T, T), F32),
            pltpu.VMEM((NZH, 4, T, T), F32),
            pltpu.VMEM((NZH, 3, T, T), BF),
            pltpu.VMEM((NZH, 3, T, T), BF),
            pltpu.VMEM((2, T, T), BF),
            pltpu.VMEM((2, T, T), BF),
            pltpu.VMEM((N_REP + 1, T, T), BF),
            pltpu.VMEM((3, 7, T, T), BF),
            pltpu.VMEM((3, 7, T, T), BF),
            pltpu.VMEM((2, NY, T, T), BF),
            pltpu.VMEM((2, NY, T, T), BF),
            pltpu.VMEM((2, T, T), BF),
            pltpu.VMEM((2, T, T), BF),
            pltpu.VMEM((2, NX, T // 8, 2 * T), F32),
            pltpu.VMEM((7, T // 8, 2 * T), F32),
            pltpu.VMEM((NY, T // 8, 2 * T), F32),
            pltpu.VMEM((NZL, T // 8, 2 * T), F32),
            pltpu.VMEM((NZH, T // 8, 2 * T), F32),
            pltpu.VMEM((2, NX, T // 8, 2 * T), F32),
            dma((7,)), dma((2,)), dma((3, 7)), dma((2, NY)), dma((N_WIDE,)),
            dma((NZH,)), dma((NZH,)), dma((NZH, 3)), dma((NZH, 3)), dma((2,)), dma((2,)),
            dma((23,)), dma((N_REP,)), dma((3, 7)), dma((3, 7)), dma((2, NY)), dma((2, NY)),
            dma((2,)), dma((2,)), dma((26,)), dma((30,)),
        ],
        compiler_params=pltpu.CompilerParams(
            collective_id=0, has_side_effects=True, vmem_limit_bytes=48 * 1024 * 1024
        ),
        name="graph_layer",
    )(*(
        pltpu.with_memory_space_constraint(value, pltpu.HBM)
        for value in (
            features, weight, cotangent,
            tile_values.reshape(N_WIDE, KT, T, T),
            tile_rows[0, 0].T, tile_counts.reshape(1, N_WIDE),
        )
    ))


def solution(mesh):
    in_specs = (
        P(("wide", "rep"), None),
        P(),
        P(("wide", "rep"), None),
        P("wide", "rep", None, None, None, None),
        P("wide", "rep", None, None),
        P("wide", "rep", None),
    )
    out_specs = (P(("wide", "rep"), None), P(), P(("wide", "rep"), None))
    return jax.shard_map(shards, mesh=mesh, in_specs=in_specs, out_specs=out_specs, check_vma=False)
```

```python
import math

import jax
import jax.numpy as jnp
from jax import lax
from jax.experimental import pallas as pl
from jax.experimental.pallas import tpu as pltpu
from jax.sharding import PartitionSpec as P

MESH = pl.DeviceIdType.MESH
T = 128
NY, NZL, NZH, NX = 8, 4, 3, 4
N_WIDE, N_REP, KT = 32, 24, 4
BF = jnp.bfloat16
F32 = jnp.float32
X_ORDER = (2, 1, 3)
NEAR, FAR = (-2, 2, -1, 1), (-3, 3, 4)
STEPS = (
    [(0, 0)] + [(0, dy) for dy in NEAR] + [(2, 0), (1, 0), (3, 0)] + [(0, dy) for dy in FAR]
    + [(line, dy) for line in (2, 1, 3) for dy in NEAR]
    + [(line, dy) for line in (2, 1, 3) for dy in FAR]
)


def place():
    wide = lax.axis_index("wide")
    rep = lax.axis_index("rep")
    y, zl = lax.rem(wide, NY), wide // NY
    core, x, zh = lax.rem(rep, 2), lax.rem(rep // 2, NX), rep // (2 * NX)
    return x, y, zl, zh, core


def kernel(
    feat_hbm, weight_hbm, cot_hbm, tiles_hbm, rows_hbm, counts_hbm,
    out_ref, wgrad_ref, fgrad_ref,
    weight, cot, rows, counts, table_v, table, tiles, xs, tot, sib_s, sib_r, x_s, x_r, z_s, z_r, g, y_s, y_r, h_s, h_r, f_s, f_r,
    w_t, w_r, w_c, w_d, w_e, w_o,
    load_sems, ag_zs, ag_ys, ag_hs, ag_r, sib_ss, sib_rs, x_ss, x_rs, z_ss, z_rs,
    g_ss, g_rs, y_ss, y_rs, h_ss, h_rs, f_ss, f_rs, w_ss, w_rs,
):
    x, y, zl, zh, core = place()

    def dev(x=x, y=y, zl=zl, zh=zh, core=core):
        return (zl * NY + y, zh * (2 * NX) + x * 2 + core)

    def up(v, by, n):
        return lax.rem(v + by, n)

    sibling = dev(core=1 - core)

    def send(src, dst, ss, rs, to):
        pltpu.make_async_remote_copy(
            src_ref=src, dst_ref=dst, send_sem=ss, recv_sem=rs,
            device_id=to, device_id_type=MESH,
        ).start()

    def wait_recv(dst, rs):
        pltpu.make_async_remote_copy(
            src_ref=dst, dst_ref=dst, send_sem=rs, recv_sem=rs,
            device_id=sibling, device_id_type=MESH,
        ).wait_recv()

    def wait_send(src, ss):
        pltpu.make_async_remote_copy(
            src_ref=src, dst_ref=src, send_sem=ss, recv_sem=ss,
            device_id=sibling, device_id_type=MESH,
        ).wait_send()

    own = zl * NY + y
    loads = [
        pltpu.make_async_copy(src, dst, load_sems.at[n])
        for n, (src, dst) in enumerate((
            (feat_hbm, xs.at[own]), (tiles_hbm, tiles), (weight_hbm, weight), (cot_hbm, cot),
            (rows_hbm, rows), (counts_hbm, counts),
        ))
    ]
    for load in loads:
        load.start()

    h_r[1] = jnp.zeros((NY, T, T), BF)
    f_r[1] = jnp.zeros((T, T), BF)
    barrier = pltpu.get_barrier_semaphore()
    chips = [(dx, dc) for dx in range(NX) for dc in range(2) if dx or dc]
    around = [dev(x=up(x, dx, NX), core=lax.rem(core + dc, 2)) for dx, dc in chips]
    partners = list(around)
    partners += [dev(y=up(y, d, NY)) for d in range(1, NY)]
    partners += [dev(zl=up(zl, d, NZL)) for d in range(1, NZL)]
    partners += [dev(zh=up(zh, d, NZH)) for d in range(1, NZH)]
    for partner in partners:
        pl.semaphore_signal(barrier, inc=1, device_id=partner, device_id_type=MESH)

    loads[4].wait()
    loads[5].wait()
    fill_table(rows, counts, table_v)
    table_load = pltpu.make_async_copy(table_v, table, load_sems.at[6])
    table_load.start()
    tot[N_WIDE * KT] = jnp.zeros((T, T), F32)
    g[N_REP] = jnp.zeros((T, T), BF)
    loads[0].wait()
    pl.semaphore_wait(barrier, len(partners))

    y_up, y_down = dev(y=up(y, 1, NY)), dev(y=up(y, NY - 1, NY))
    y_up2, y_down2 = dev(y=up(y, 2, NY)), dev(y=up(y, NY - 2, NY))

    mid = (zl == 1) | (zl == 2)
    even = lax.rem(y, 2) == 0
    lines = (zl, zl + 1 - 2 * lax.rem(zl, 2), up(zl, 2, NZL), NZL - 1 - zl)
    own_line, pair, across, other = range(4)

    def block(line, dy):
        return lines[line] * NY + up(y, (dy + NY) % NY, NY)

    def y_pass(line, n, c, to):
        i = (own_line, across, other).index(line)
        send(xs.at[c], xs.at[c], ag_ys.at[i, n], ag_r.at[c], to)

    def z_pass(dy):
        c = block(own_line, dy)
        send(xs.at[c], xs.at[c], ag_hs.at[0, dy % NY], ag_r.at[c], dev(zl=lines[pair]))

        @pl.when(mid)
        def _():
            send(xs.at[c], xs.at[c], ag_hs.at[1, dy % NY], ag_r.at[c], dev(zl=lines[other]))

    def spread(line):
        c = block(line, 0)
        for n, to in enumerate((y_up2, y_down2, y_up, y_down)):
            y_pass(line, n, c, to)

    def have(line, dy):
        c = block(line, dy)
        wait_recv(xs.at[c], ag_r.at[c])

    def onward(line):
        have(line, -2)
        below = block(line, -2)
        y_pass(line, 4, below, y_up)

        @pl.when(even)
        def _():
            y_pass(line, 6, below, y_up2)

        have(line, 2)
        above = block(line, 2)
        y_pass(line, 5, above, y_down)

        @pl.when(jnp.logical_not(even))
        def _():
            y_pass(line, 6, above, y_down2)

    send(xs.at[own], xs.at[own], ag_zs.at[0], ag_r.at[own], dev(zl=lines[across]))

    @pl.when(jnp.logical_not(mid))
    def _():
        send(xs.at[own], xs.at[own], ag_zs.at[1], ag_r.at[own], dev(zl=lines[other]))

    spread(own_line)
    z_pass(0)
    table_load.wait()
    loads[1].wait()

    def process(rank, c):
        product = jnp.dot(
            tiles[c].reshape(KT * T, T), xs[c], preferred_element_type=F32
        )
        for k in range(KT):
            before = table[k, c]
            tot[rank * KT + k] = product[k * T:(k + 1) * T] + tot[before]

    def work(first, items):
        for n, (line, dy) in enumerate(items):
            process(first + n, block(line, dy))

    process(0, own)
    onward(own_line)
    z_pass(-2)
    z_pass(2)
    have(across, 0)
    spread(across)

    @pl.when(jnp.logical_not(mid))
    def _():
        have(other, 0)
        spread(other)

    have(own_line, -1)
    z_pass(-1)
    have(own_line, 1)
    z_pass(1)
    work(1, STEPS[1:5])
    have(pair, 0)

    @pl.when(mid)
    def _():
        have(other, 0)

    onward(across)
    for dy in (-3, 3, 4):
        have(own_line, dy)
        z_pass(dy)
    work(5, STEPS[5:11])
    have(across, -1)
    have(across, 1)
    work(11, STEPS[11:15])
    for dy in (-2, 2, -1, 1):
        have(pair, dy)
    work(15, STEPS[15:19])

    for n, dy in enumerate(FAR):
        have(across, dy)
        c = block(across, dy)

        @pl.when(mid)
        def _():
            send(xs.at[c], xs.at[c], ag_hs.at[2, n], ag_r.at[c], dev(zl=lines[pair]))

    for dy in NEAR:
        have(other, dy)
    work(19, STEPS[19:23])
    work(23, STEPS[23:26])
    for first, line in ((26, pair), (29, other)):
        for dy in FAR:
            have(line, dy)
        work(first, STEPS[first:first + 3])

    def part(zh_to, x_to, core_to):
        r = zh_to * (2 * NX) + x_to * 2 + core_to
        return tot[table[2 * KT, r]]

    turns = (1, 2, 0)
    for m in turns:
        q = up(zh, m, NZH)
        for n, dx in enumerate(X_ORDER + (0,)):
            sib_s[m, n] = part(q, up(x, dx, NX), 1 - core)
        send(sib_s.at[m], sib_r.at[m], sib_ss.at[m], sib_rs.at[m], sibling)
    for m in turns:
        q = up(zh, m, NZH)
        wait_recv(sib_r.at[m], sib_rs.at[m])
        for n, dx in enumerate(X_ORDER):
            to = up(x, dx, NX)
            x_s[m, n] = (part(q, to, core) + sib_r[m, n]).astype(BF)
            send(x_s.at[m, n], x_r.at[m, n], x_ss.at[m, n], x_rs.at[m, n], dev(x=to))

    def column_sum(m):
        value = part(up(zh, m, NZH), x, core) + sib_r[m, 3]
        for n in range(3):
            wait_recv(x_r.at[m, n], x_rs.at[m, n])
            value = value + x_r[m, n].astype(F32)
        return value

    for n in range(2):
        z_s[n] = column_sum(n + 1).astype(BF)
        send(z_s.at[n], z_r.at[n], z_ss.at[n], z_rs.at[n], dev(zh=up(zh, n + 1, NZH)))
    total = column_sum(0)
    for n in range(2):
        wait_recv(z_r.at[n], z_rs.at[n])
        total = total + z_r[n].astype(F32)

    loads[2].wait()
    loads[3].wait()
    agg = total.astype(BF)
    hidden = jnp.dot(agg, weight[...], preferred_element_type=F32)
    sig = jax.nn.sigmoid(hidden)
    grad_hidden = (cot[...].astype(F32) * (sig * (1.0 + hidden * (1.0 - sig)))).astype(BF)
    grad_t = lax.dot_general(
        weight[...], grad_hidden, (((1,), (1,)), ((), ())), preferred_element_type=F32
    )
    mine = zh * (2 * NX) + x * 2 + core
    g[mine] = grad_t.astype(BF)

    def g_send(n, r, to):
        send(g.at[r], g.at[r], g_ss.at[n], g_rs.at[r], to)

    for n in range(2):
        g_send(n, mine, dev(zh=up(zh, n + 1, NZH)))
    for n, dx in enumerate(X_ORDER):
        g_send(2 + n, mine, dev(x=up(x, dx, NX)))
    g_send(5, mine, sibling)

    out_ref[...] = (hidden * sig).astype(BF)
    term_of_weight = lax.dot_general(
        agg, grad_hidden, (((0,), (0,)), ((), ())), preferred_element_type=F32
    )
    for i in range(2):
        for j in range(NX):
            row = (i * NX + j) * (T // 8)
            w_t[i, j] = term_of_weight[row:row + T // 8]
    for n, (dx, dc) in enumerate(chips):
        part_for = w_t.at[lax.rem(core + dc, 2), up(x, dx, NX)]
        send(part_for, w_r.at[n], w_ss.at[n], w_rs.at[n], around[n])

    early = (jnp.where(zh == 2, 1, 2), jnp.where(zh == 0, 1, 0))

    def from_z(n):
        r = early[n] * (2 * NX) + x * 2 + core
        wait_recv(g.at[r], g_rs.at[r])
        for m, dx in enumerate(X_ORDER):
            g_send(6 + 4 * n + m, r, dev(x=up(x, dx, NX)))
        g_send(6 + 4 * n + 3, r, sibling)

    def from_x(q, at):
        for n, dx in enumerate(X_ORDER):
            r = at * (2 * NX) + up(x, NX - dx, NX) * 2 + core
            wait_recv(g.at[r], g_rs.at[r])
            g_send(14 + 3 * q + n, r, sibling)

    def spread_sum(buf, base, me, n):
        for i in range(n):
            @pl.when(me != i)
            def _():
                wait_recv(buf.at[i], w_rs.at[base + i])
        value = buf[0]
        for i in range(1, n):
            value = value + buf[i]
        return value

    from_z(0)
    w_sum = w_t[core, x]
    for n in range(7):
        wait_recv(w_r.at[n], w_rs.at[n])
        w_sum = w_sum + w_r[n]
    w_c[y] = w_sum
    for n in range(1, NY):
        send(w_c.at[y], w_c.at[y], w_ss.at[6 + n], w_rs.at[7 + y], dev(y=up(y, n, NY)))
    from_z(1)
    from_x(0, zh)
    from_x(1, early[0])
    w_d[zl] = spread_sum(w_c, 7, y, NY)
    for n in range(1, NZL):
        send(w_d.at[zl], w_d.at[zl], w_ss.at[13 + n], w_rs.at[15 + zl], dev(zl=up(zl, n, NZL)))
    from_x(2, early[1])

    def sib_wait(n, carry):
        r = n * 2 + 1 - core
        wait_recv(g.at[r], g_rs.at[r])
        return carry

    lax.fori_loop(0, N_REP // 2, sib_wait, 0)

    def term(c):
        left = jnp.concatenate(
            [g[table[KT + k, c]] for k in range(KT)], axis=1
        )
        return jnp.dot(left, tiles[c].reshape(KT * T, T), preferred_element_type=F32)

    def y_send(line, n, value, to):
        i = (own_line, across, other).index(line)
        y_s[i, n] = value.astype(BF)
        send(y_s.at[i, n], y_r.at[i, n], y_ss.at[i, n], y_rs.at[i, n], to)

    def y_have(line, n):
        i = (own_line, across, other).index(line)
        wait_recv(y_r.at[i, n], y_rs.at[i, n])
        return y_r[i, n].astype(F32)

    def hop(slot, line, dy):
        k = dy % NY
        h_s[slot, k] = term(block(line, dy)).astype(BF)
        send(h_s.at[slot, k], h_r.at[slot, k], h_ss.at[slot, k], h_rs.at[slot, k], dev(zl=lines[line]))

    def value_of(line, dy):
        value = term(block(line, dy))
        if line == own_line:
            k = dy % NY
            wait_recv(h_r.at[0, k], h_rs.at[0, k])
            value = value + h_r[0, k].astype(F32)

            @pl.when(mid)
            def _():
                wait_recv(h_r.at[1, k], h_rs.at[1, k])

            value = value + jnp.where(mid, h_r[1, k].astype(F32), 0.0)
        return value

    def outer_part(line):
        value = value_of(line, 4)

        @pl.when(even)
        def _():
            y_send(line, 0, value, y_up2)

        @pl.when(jnp.logical_not(even))
        def _():
            y_send(line, 0, value, y_down2)

        above, below = value_of(line, 3), value_of(line, -3)
        y_send(line, 1, above, y_up)
        y_send(line, 2, below, y_down)

    def next_part(line):
        above, below = value_of(line, 1), value_of(line, -1)
        y_send(line, 3, above, y_up)
        y_send(line, 4, below, y_down)

    def second_part(line):
        above, below = value_of(line, 2), value_of(line, -2)
        above = above + y_have(line, 1)
        below = below + y_have(line, 2)
        four = y_have(line, 0)
        y_send(line, 5, above + jnp.where(even, four, 0.0), y_up2)
        y_send(line, 6, below + jnp.where(even, 0.0, four), y_down2)

    def whole(line):
        value = value_of(line, 0)
        for n in range(3, 7):
            value = value + y_have(line, n)
        return value

    def z_send(n, line):
        f_s[n] = whole(line).astype(BF)
        send(f_s.at[n], f_r.at[n], f_ss.at[n], f_rs.at[n], dev(zl=lines[line]))

    for dy in FAR:
        hop(0, pair, dy)

    @pl.when(mid)
    def _():
        for dy in FAR:
            hop(1, other, dy)

    outer_part(across)

    @pl.when(jnp.logical_not(mid))
    def _():
        outer_part(other)

    for dy in NEAR + (0,):
        hop(0, pair, dy)

    @pl.when(mid)
    def _():
        for dy in NEAR + (0,):
            hop(1, other, dy)

    outer_part(own_line)

    w_e[zh] = spread_sum(w_d, 15, zl, NZL)
    for n in range(1, NZH):
        send(w_e.at[zh], w_e.at[zh], w_ss.at[16 + n], w_rs.at[19 + zh], dev(zh=up(zh, n, NZH)))

    second_part(across)

    @pl.when(jnp.logical_not(mid))
    def _():
        second_part(other)

    next_part(across)

    @pl.when(jnp.logical_not(mid))
    def _():
        next_part(other)

    next_part(own_line)

    w_o[core, x] = spread_sum(w_e, 19, zh, NZH) * (1.0 / math.sqrt(N_WIDE * N_REP * T))
    for n in range(7):
        send(w_o.at[core, x], w_o.at[core, x], w_ss.at[19 + n], w_rs.at[22 + core * NX + x], around[n])

    second_part(own_line)
    z_send(0, across)

    @pl.when(jnp.logical_not(mid))
    def _():
        z_send(1, other)

    value = whole(own_line)

    wait_recv(f_r.at[0], f_rs.at[0])
    value = value + f_r[0].astype(F32)

    @pl.when(jnp.logical_not(mid))
    def _():
        wait_recv(f_r.at[1], f_rs.at[1])

    value = value + jnp.where(mid, 0.0, f_r[1].astype(F32))
    fgrad_ref[...] = value.T.astype(BF)
    for n, (dx, dc) in enumerate(chips):
        i, j = lax.rem(core + dc, 2), up(x, dx, NX)
        wait_recv(w_o.at[i, j], w_rs.at[22 + i * NX + j])
    wgrad_ref[...] = w_o[...].reshape(T, 2 * T)

    def settle(n, carry):
        wait_send(xs.at[0], ag_hs.at[0, n])
        wait_send(h_s.at[0, n], h_ss.at[0, n])

        @pl.when(mid)
        def _():
            wait_send(xs.at[0], ag_hs.at[1, n])
            wait_send(h_s.at[1, n], h_ss.at[1, n])

        return carry

    lax.fori_loop(0, NY, settle, 0)

    def drain(n, carry):
        for i in range(2):
            wait_send(xs.at[0], ag_ys.at[i, n])
            wait_send(y_s.at[i, n], y_ss.at[i, n])

        @pl.when(jnp.logical_not(mid))
        def _():
            wait_send(y_s.at[2, n], y_ss.at[2, n])

        return carry

    lax.fori_loop(0, 7, drain, 0)

    @pl.when(mid)
    def _():
        for n in range(len(FAR)):
            wait_send(xs.at[0], ag_hs.at[2, n])

    @pl.when(jnp.logical_not(mid))
    def _():
        for n in range(4):
            wait_send(xs.at[0], ag_ys.at[2, n])

    wait_send(xs.at[0], ag_zs.at[0])
    wait_send(f_s.at[0], f_ss.at[0])

    @pl.when(jnp.logical_not(mid))
    def _():
        wait_send(xs.at[0], ag_zs.at[1])
        wait_send(f_s.at[1], f_ss.at[1])

    for n in range(2):
        wait_send(z_s.at[n], z_ss.at[n])
    for m in range(NZH):
        wait_send(sib_s.at[m], sib_ss.at[m])
        for n in range(3):
            wait_send(x_s.at[m, n], x_ss.at[m, n])

    def drain_g(n, carry):
        wait_send(g.at[0], g_ss.at[n])
        return carry

    lax.fori_loop(0, 23, drain_g, 0)

    def drain_w(n, carry):
        wait_send(w_r.at[0], w_ss.at[n])
        return carry

    lax.fori_loop(0, 26, drain_w, 0)


def rank_of(c):
    x, y, zl, zh, core = place()
    v = c // NY
    line = jnp.where(v == zl, 0, jnp.where(v == NZL - 1 - zl, 3, jnp.where(lax.rem(v + zl, 2) == 0, 2, 1)))
    dy = lax.rem(lax.rem(c, NY) - y + NY, NY)
    rank = jnp.zeros_like(c)
    for n, (on, at) in enumerate(STEPS):
        rank = jnp.where((line == on) & (dy == at % NY), n, rank)
    return rank


def fill_table(rows, counts, table_v):
    square = (N_WIDE, N_WIDE)
    lane = lax.broadcasted_iota(jnp.int32, square, 1)
    sub = lax.broadcasted_iota(jnp.int32, square, 0)
    rank_l, rank_s = rank_of(lane), rank_of(sub)
    live = counts[...]
    code = [jnp.where(live > k, rows[k:k + 1, :], -1) for k in range(KT)]
    code_l = [jnp.broadcast_to(v, square) for v in code]
    code_s = [
        jnp.broadcast_to(
            jnp.max(jnp.where(lane == sub, v, -1), axis=1, keepdims=True), square
        )
        for v in code_l
    ]
    none = N_WIDE * KT

    def best(matches):
        keys = [jnp.where(m, rank_s * KT + k, -1) for k, m in enumerate(matches)]
        top = keys[0]
        for key in keys[1:]:
            top = jnp.maximum(top, key)
        top = jnp.max(top, axis=0, keepdims=True)
        return jnp.where(top < 0, none, top)

    for k in range(KT):
        table_v[k:k + 1, 0:N_WIDE] = best(
            [(v == code_l[k]) & (rank_s < rank_l) & (v >= 0) for v in code_s]
        )
        table_v[KT + k:KT + k + 1, 0:N_WIDE] = jnp.where(code[k] < 0, N_REP, code[k])
    table_v[2 * KT:2 * KT + 1, 0:N_WIDE] = best([v == lane for v in code_s])


def shards(features, weight, cotangent, tile_values, tile_rows, tile_counts):
    dma = pltpu.SemaphoreType.DMA
    hbm = pl.BlockSpec(memory_space=pltpu.HBM)
    vmem = pl.BlockSpec(memory_space=pltpu.VMEM)
    shapes = (
        jax.ShapeDtypeStruct((T, 2 * T), BF),
        jax.ShapeDtypeStruct((T, 2 * T), F32),
        jax.ShapeDtypeStruct((T, T), BF),
    )
    return pl.pallas_call(
        kernel,
        out_shape=shapes,
        in_specs=[hbm] * 6,
        out_specs=(vmem, vmem, vmem),
        scratch_shapes=[
            pltpu.VMEM((T, 2 * T), BF),
            pltpu.VMEM((T, 2 * T), BF),
            pltpu.VMEM((KT, N_WIDE), jnp.int32),
            pltpu.VMEM((1, N_WIDE), jnp.int32),
            pltpu.VMEM((16, T), jnp.int32),
            pltpu.SMEM((16, T), jnp.int32),
            pltpu.VMEM((N_WIDE, KT, T, T), BF),
            pltpu.VMEM((N_WIDE, T, T), BF),
            pltpu.VMEM((N_WIDE * KT + 1, T, T), F32),
            pltpu.VMEM((NZH, 4, T, T), F32),
            pltpu.VMEM((NZH, 4, T, T), F32),
            pltpu.VMEM((NZH, 3, T, T), BF),
            pltpu.VMEM((NZH, 3, T, T), BF),
            pltpu.VMEM((2, T, T), BF),
            pltpu.VMEM((2, T, T), BF),
            pltpu.VMEM((N_REP + 1, T, T), BF),
            pltpu.VMEM((3, 7, T, T), BF),
            pltpu.VMEM((3, 7, T, T), BF),
            pltpu.VMEM((2, NY, T, T), BF),
            pltpu.VMEM((2, NY, T, T), BF),
            pltpu.VMEM((2, T, T), BF),
            pltpu.VMEM((2, T, T), BF),
            pltpu.VMEM((2, NX, T // 8, 2 * T), F32),
            pltpu.VMEM((7, T // 8, 2 * T), F32),
            pltpu.VMEM((NY, T // 8, 2 * T), F32),
            pltpu.VMEM((NZL, T // 8, 2 * T), F32),
            pltpu.VMEM((NZH, T // 8, 2 * T), F32),
            pltpu.VMEM((2, NX, T // 8, 2 * T), F32),
            dma((7,)), dma((2,)), dma((3, 7)), dma((3, NY)), dma((N_WIDE,)),
            dma((NZH,)), dma((NZH,)), dma((NZH, 3)), dma((NZH, 3)), dma((2,)), dma((2,)),
            dma((23,)), dma((N_REP,)), dma((3, 7)), dma((3, 7)), dma((2, NY)), dma((2, NY)),
            dma((2,)), dma((2,)), dma((26,)), dma((30,)),
        ],
        compiler_params=pltpu.CompilerParams(
            collective_id=0, has_side_effects=True, vmem_limit_bytes=48 * 1024 * 1024
        ),
        name="graph_layer",
    )(*(
        pltpu.with_memory_space_constraint(value, pltpu.HBM)
        for value in (
            features, weight, cotangent,
            tile_values.reshape(N_WIDE, KT, T, T),
            tile_rows[0, 0].T, tile_counts.reshape(1, N_WIDE),
        )
    ))


def solution(mesh):
    in_specs = (
        P(("wide", "rep"), None),
        P(),
        P(("wide", "rep"), None),
        P("wide", "rep", None, None, None, None),
        P("wide", "rep", None, None),
        P("wide", "rep", None),
    )
    out_specs = (P(("wide", "rep"), None), P(), P(("wide", "rep"), None))
    return jax.shard_map(shards, mesh=mesh, in_specs=in_specs, out_specs=out_specs, check_vma=False)
```
